32 devices in a mesh: seq: 16 (over z, y, x), head: 2 (over core).
Axes of the slice: x: 2, y: 2, z: 4, core: 2. Of those that a mesh axis runs over, the one named last changes fastest.
Arguments:
- stream_in: bfloat16 [2048, 2048], P('seq'), may hold values from -6 to 6
- doc_start: int32 [2048], P('seq'), may hold values from 0 to 2047, as said below
- first_gain: float32 [2048], replicated, may hold values from 0.5 to 1.5
- w_query: bfloat16 [2048, 2048], P('seq', 'head'), may hold values from -0.125 to 0.125
- w_key: bfloat16 [2048, 2048], P('seq', 'head'), may hold values from -0.125 to 0.125
- w_value: bfloat16 [2048, 4096], P('seq', 'head'), may hold values from -0.125 to 0.125
- w_outgate: bfloat16 [2048, 4096], P('seq', 'head'), may hold values from -0.125 to 0.125
- w_decay: bfloat16 [2048, 8], P('seq', 'head'), may hold values from -0.125 to 0.125
- w_rate: bfloat16 [2048, 8], P('seq', 'head'), may hold values from -0.125 to 0.125
- conv_query: float32 [4, 2048], P(None, 'head'), may hold values from -3 to 3
- conv_key: float32 [4, 2048], P(None, 'head'), may hold values from -3 to 3
- conv_value: float32 [4, 4096], P(None, 'head'), may hold values from -3 to 3
- a_log: float32 [8], P('head'), may hold values from -1 to 1.5
- dt_bias: float32 [8], P('head'), may hold values from -6 to -2
- out_gain: float32 [512], replicated, may hold values from 0.5 to 1.5
- w_out: bfloat16 [4096, 2048], P('head', 'seq'), may hold values from -0.1875 to 0.1875
- second_gain: float32 [2048], replicated, may hold values from 0.5 to 1.5
- w_gate: bfloat16 [2048, 5632], P('seq', 'head'), may hold values from -0.125 to 0.125
- w_up: bfloat16 [2048, 5632], P('seq', 'head'), may hold values from -0.125 to 0.125
- w_down: bfloat16 [5632, 2048], P('head', 'seq'), may hold values from -0.078125 to 0.078125
- cotangent: bfloat16 [2048, 2048], P('seq'), may hold values from -6 to 6
Outputs:
- output: bfloat16 [2048, 2048], P('seq')
- grad_input: float32 [2048, 2048], P('seq')
- grad_first_gain: float32 [2048], replicated
- grad_w_query: float32 [2048, 2048], P('seq', 'head')
- grad_w_key: float32 [2048, 2048], P('seq', 'head')
- grad_w_value: float32 [2048, 4096], P('seq', 'head')
- grad_w_outgate: float32 [2048, 4096], P('seq', 'head')
- grad_w_decay: float32 [2048, 8], P('seq', 'head')
- grad_w_rate: float32 [2048, 8], P('seq', 'head')
- grad_conv_query: float32 [4, 2048], P(None, 'head')
- grad_conv_key: float32 [4, 2048], P(None, 'head')
- grad_conv_value: float32 [4, 4096], P(None, 'head')
- grad_a_log: float32 [8], P('head')
- grad_dt_bias: float32 [8], P('head')
- grad_out_gain: float32 [512], replicated
- grad_w_out: float32 [4096, 2048], P('head', 'seq')
- grad_second_gain: float32 [2048], replicated
- grad_w_gate: float32 [2048, 5632], P('seq', 'head')
- grad_w_up: float32 [2048, 5632], P('seq', 'head')
- grad_w_down: float32 [5632, 2048], P('head', 'seq')
The draws below stay inside these ranges and needn't reach their ends.
Inputs may be any that keep to these rules, and one draw needn't show every extreme that they name: doc_start never falls along the stream, doc_start[t] <= t, and doc_start[t] = t where a document begins; positions 0 and 2047 each begin one; every document has at most 1024 tokens, and one has exactly 1024.
All inputs are finite; a program needn't handle non-finite values.
Results may differ from the reference program's by a relative error of at most 0.012.
Values may be sent and summed in bfloat16 or wider, within the bound.
No kernel may reach another device: no remote copies, remote signals or barrier semaphores. Data moves between devices by JAX's collectives and lax.ppermute only.
A program may use at most 640 MiB of HBM per device.

```python
import jax
import jax.numpy as jnp
from jax import lax

D = 2048
H = 8
DV = 512
FF = 5632
KC = 4
GROUP = 64
TOK_DEV = 128
HK = 2048
HV = 4096
TOKENS = 2048


def draw_doc_start(key, part):
    key = jax.random.fold_in(key, 7)
    key_cut, key_after, key_extra = jax.random.split(key, 3)
    places = jnp.arange(TOKENS, dtype=jnp.int32)
    devices_along = TOKENS // TOK_DEV
    half_count = devices_along // 2
    long_cut = jax.random.randint(key_cut, (), 2, half_count - 2)
    long_begin = long_cut * TOK_DEV
    long_end = long_begin + TOKENS // 2
    near_begin = long_end + TOK_DEV + jax.random.randint(key_after, (), 1, 4)
    extra_starts = jax.random.randint(key_extra, (TOKENS,), 0, TOK_DEV) == 0
    early_zone = (places >= TOK_DEV + TOK_DEV // 2) & (places < long_begin)
    late_zone = (places > near_begin) & (places < TOKENS - TOK_DEV - TOK_DEV // 2)
    begins = (places == 0) | (places == long_begin) | (places == long_end) | (places == near_begin) | (places == TOKENS - 1) | extra_starts & (early_zone | late_zone)
    return lax.cummax(jnp.where(begins, places, 0), axis=0)


def block_scale(own_key, shape, cuts, least, high):
    gain, own = 1.0, jax.random.fold_in(own_key, 6)
    for position, shards_of in cuts:
        steps = jnp.exp(jax.random.uniform(jax.random.fold_in(own, position), (shards_of,), jnp.float32, least / len(cuts), high / len(cuts)))
        gain = gain * jnp.repeat(steps, shape[position] // shards_of).reshape([-1 if axis == position else 1 for axis in range(len(shape))])
    return gain


def gaussian(rng, dims, scale, bound, shards=(), held_as=jnp.bfloat16):
    loudness = block_scale(rng, dims, shards, -0.22, 0.18) if shards else 1.0
    values = jax.random.normal(rng, dims, jnp.float32) * scale * loudness
    return jnp.minimum(jnp.maximum(values, -bound), bound).astype(held_as)


def setup_inputs(seed: int = 0) -> dict:
    arg_keys = jax.random.split(jax.random.key(seed), 22)
    return {
        "stream_in": gaussian(arg_keys[0], (TOKENS, D), 1.0, 6.0, ((0, 16),)),
        "doc_start": draw_doc_start(jax.random.fold_in(arg_keys[21], 71), 0),
        "first_gain": jnp.clip(1.0 + 0.1 * jax.random.normal(arg_keys[2], (D,), jnp.float32), 0.5, 1.5),
        "w_query": gaussian(arg_keys[3], (D, HK), D ** -0.5, 0.125, ((0, 16), (1, 2))),
        "w_key": gaussian(arg_keys[4], (D, HK), D ** -0.5, 0.125, ((0, 16), (1, 2))),
        "w_value": gaussian(arg_keys[5], (D, HV), D ** -0.5, 0.125, ((0, 16), (1, 2))),
        "w_outgate": gaussian(arg_keys[6], (D, HV), D ** -0.5, 0.125, ((0, 16), (1, 2))),
        "w_decay": gaussian(arg_keys[7], (D, H), D ** -0.5, 0.125, ((0, 16), (1, 2))),
        "w_rate": gaussian(arg_keys[8], (D, H), D ** -0.5, 0.125, ((0, 16), (1, 2))),
        "conv_query": gaussian(arg_keys[9], (KC, HK), KC ** -0.5, 3.0, ((1, 2),), jnp.float32),
        "conv_key": gaussian(arg_keys[10], (KC, HK), KC ** -0.5, 3.0, ((1, 2),), jnp.float32),
        "conv_value": gaussian(arg_keys[11], (KC, HV), KC ** -0.5, 3.0, ((1, 2),), jnp.float32),
        "a_log": jnp.clip(-1.0 + 2.5 * jax.random.uniform(arg_keys[12], (H,), jnp.float32) ** block_scale(arg_keys[12], (H,), ((0, 2),), -0.2, 0.2), -1.0, 1.5),
        "dt_bias": jnp.clip(-6.0 + 4.0 * jax.random.uniform(arg_keys[13], (H,), jnp.float32) ** block_scale(arg_keys[13], (H,), ((0, 2),), -0.2, 0.2), -6.0, -2.0),
        "out_gain": jnp.clip(1.0 + 0.1 * jax.random.normal(arg_keys[14], (DV,), jnp.float32), 0.5, 1.5),
        "w_out": gaussian(arg_keys[15], (HV, D), (HV // 4) ** -0.5, 0.1875, ((0, 2), (1, 16))),
        "second_gain": jnp.clip(1.0 + 0.1 * jax.random.normal(arg_keys[16], (D,), jnp.float32), 0.5, 1.5),
        "w_gate": gaussian(arg_keys[17], (D, FF), D ** -0.5, 0.125, ((0, 16), (1, 2))),
        "w_up": gaussian(arg_keys[18], (D, FF), D ** -0.5, 0.125, ((0, 16), (1, 2))),
        "w_down": gaussian(arg_keys[19], (FF, D), FF ** -0.5, 0.078125, ((0, 2), (1, 16))),
        "cotangent": gaussian(arg_keys[20], (TOKENS, D), 1.0, 6.0, ((0, 16),)),
    }


highest = lax.Precision.HIGHEST

@jax.custom_vjp
def low(v):
    return lax.optimization_barrier(v.astype(jnp.bfloat16)).astype(jnp.float32)

@jax.custom_vjp
def low_back(v):
    return v

def low_keep(v):
    return (low(v), None)

def low_pass(kept, grad):
    return (grad,)

def back_keep(v):
    return (v, None)

def back_low(kept, grad):
    return (low(grad),)
low.defvjp(low_keep, low_pass)
low_back.defvjp(back_keep, back_low)

def rms_norm(values, eps):
    return values * lax.rsqrt(lax.optimization_barrier(jnp.mean(values * values, axis=-1, keepdims=True)) + eps)

def block_step(carried, pieces):
    q, k, values, write_rate, log_decay, starts, places = pieces
    cumulated = jnp.cumsum(log_decay, axis=0)
    keep_mask = (starts[:, None] <= places[None, :]) & (places[:, None] >= places[None, :])
    strict_mask = keep_mask & (places[:, None] > places[None, :])
    gap_log = cumulated[:, None, :] - cumulated[None, :, :]
    fading = jnp.exp(jnp.where(keep_mask[:, :, None], gap_log, -10000.0))
    fading = jnp.transpose(fading, (2, 0, 1))
    from_start = jnp.exp(cumulated) * (starts < places[0]).astype(jnp.float32)[:, None]
    key_key = jnp.einsum('thd,shd->hts', k, k, precision=highest)
    lower_part = key_key * fading * strict_mask.astype(jnp.float32)[None]
    rate_rows = write_rate.T
    system = jnp.eye(q.shape[0], dtype=jnp.float32)[None] + rate_rows[:, :, None] * lower_part
    key_state = jnp.einsum('thd,hde->hte', k, carried, precision=highest)
    right_side = rate_rows[:, :, None] * (jnp.transpose(values, (1, 0, 2)) - from_start.T[:, :, None] * key_state)
    new_values = jax.scipy.linalg.solve_triangular(system, right_side, lower=True, unit_diagonal=True)
    query_key = jnp.einsum('thd,shd->hts', q, k, precision=highest) * fading
    query_state = jnp.einsum('thd,hde->hte', q, carried, precision=highest)
    results = from_start.T[:, :, None] * query_state + jnp.einsum('hts,hse->hte', query_key, new_values, precision=highest)
    last_row = fading[:, -1, :]
    new_state = from_start[-1][:, None, None] * carried + jnp.einsum('hs,shd,hse->hde', last_row, k, new_values, precision=highest)
    return (new_state, jnp.transpose(results, (1, 0, 2)))

def run_chain(carried, q, k, values, write_rate, log_decay, starts, places):
    blocks = q.shape[0] // GROUP

    def split_rows(array):
        return array.reshape((blocks, GROUP) + array.shape[1:])
    pieces = (split_rows(q), split_rows(k), split_rows(values), split_rows(write_rate), split_rows(log_decay), split_rows(starts), split_rows(places))
    last_state, results = lax.scan(jax.checkpoint(block_step), carried, pieces)
    return (last_state, results.reshape((q.shape[0],) + results.shape[2:]))

def prepare(ext_query, ext_key, ext_value, decay_raw, rate_raw, conv_query, conv_key, conv_value, a_log, dt_bias, starts, places):
    tok_rows = decay_raw.shape[0]
    head_count = decay_raw.shape[1]
    margin = conv_query.shape[0] - 1

    def filtered(extended, weight):
        summed = jnp.zeros((tok_rows, weight.shape[1]), jnp.float32)
        for offset in range(weight.shape[0]):
            valid = (places - offset >= starts).astype(jnp.float32)[:, None]
            summed = summed + weight[offset] * extended[margin - offset:margin - offset + tok_rows] * valid
        return jax.nn.silu(summed)
    q = filtered(ext_query, conv_query).reshape(tok_rows, head_count, -1)
    k = filtered(ext_key, conv_key).reshape(tok_rows, head_count, -1)
    v = filtered(ext_value, conv_value).reshape(tok_rows, head_count, -1)
    q = q * lax.rsqrt(lax.optimization_barrier(jnp.sum(q * q, axis=-1, keepdims=True)) + 1e-06) * q.shape[2] ** (-0.5)
    k = k * lax.rsqrt(lax.optimization_barrier(jnp.sum(k * k, axis=-1, keepdims=True)) + 1e-06)
    write_rate = jax.nn.sigmoid(rate_raw)
    log_decay = -jnp.exp(a_log) * jax.nn.softplus(decay_raw + dt_bias)
    return (q, k, v, write_rate, log_decay)

def out_gate_norm(core, gate_value, out_gain):
    normed = rms_norm(core, 1e-05) * out_gain
    return normed.reshape(gate_value.shape) * jax.nn.silu(gate_value)

def reference(stream_in, doc_start, first_gain, w_query, w_key, w_value, w_outgate, w_decay, w_rate, conv_query, conv_key, conv_value, a_log, dt_bias, out_gain, w_out, second_gain, w_gate, w_up, w_down, cotangent):
    places = jnp.arange(stream_in.shape[0], dtype=jnp.int32)
    primals = tuple((a.astype(jnp.float32) for a in (stream_in, first_gain, w_query, w_key, w_value, w_outgate, w_decay, w_rate, conv_query, conv_key, conv_value, a_log, dt_bias, out_gain, w_out, second_gain, w_gate, w_up, w_down)))

    def forward(stream, first_gain, w_query, w_key, w_value, w_outgate, w_decay, w_rate, conv_query, conv_key, conv_value, a_log, dt_bias, out_gain, w_out, second_gain, w_gate, w_up, w_down):
        hidden_one = low(rms_norm(stream, 1e-06) * first_gain)

        def project(weight):
            return jnp.dot(hidden_one, weight, precision=highest)
        pre_query = low_back(low(project(w_query)))
        pre_key = low_back(low(project(w_key)))
        pre_value = low_back(low(project(w_value)))
        gate_value = low_back(project(w_outgate))
        decay_raw = project(w_decay)
        rate_raw = project(w_rate)
        margin = conv_query.shape[0] - 1

        def padded(array):
            return jnp.pad(array, ((margin, 0), (0, 0)))
        q, k, v, write_rate, log_decay = prepare(padded(pre_query), padded(pre_key), padded(pre_value), decay_raw, rate_raw, conv_query, conv_key, conv_value, a_log, dt_bias, doc_start, places)
        q, k, v = (low(q), low(k), low(v))
        zero_state = jnp.zeros((q.shape[1], q.shape[2], v.shape[2]), jnp.float32)
        last_state, core = run_chain(zero_state, q, k, v, write_rate, log_decay, doc_start, places)
        gated = low(out_gate_norm(core, gate_value, out_gain))
        middle = stream + low_back(jnp.dot(gated, w_out, precision=highest))
        hidden_two = low(rms_norm(middle, 1e-06) * second_gain)
        gate_pre = low_back(jnp.dot(hidden_two, w_gate, precision=highest))
        up_pre = low_back(jnp.dot(hidden_two, w_up, precision=highest))
        inner = low(jax.nn.silu(gate_pre) * up_pre)
        return middle + low_back(jnp.dot(inner, w_down, precision=highest))
    result, pull = jax.vjp(forward, *primals)
    grads = pull(cotangent.astype(jnp.float32))
    return (result.astype(jnp.bfloat16), grads[0], grads[1], grads[2], grads[3], grads[4], grads[5], grads[6], grads[7], grads[8], grads[9], grads[10], grads[11], grads[12], grads[13], grads[14], grads[15], grads[16], grads[17], grads[18])
```

```python
import functools

import jax
import jax.numpy as jnp
from jax import lax
from jax.experimental import pallas as pl
from jax.experimental.pallas import tpu as pltpu
from jax.sharding import PartitionSpec as P

highest = lax.Precision.HIGHEST
bf16 = jnp.bfloat16
f32 = jnp.float32


def mm(left, right):
    return jnp.dot(left, right, preferred_element_type=f32)


def mm_nt(left, right):
    return lax.dot_general(left, right, (((1,), (1,)), ((), ())), preferred_element_type=f32)


def mm_tn(left, right):
    return lax.dot_general(left, right, (((0,), (0,)), ((), ())), preferred_element_type=f32)


def exact(spec, *operands):
    return jnp.einsum(spec, *operands, precision=highest)


def gather_tokens(rows):
    return lax.all_gather(rows, ("seq", "head"), axis=0, tiled=True)


def scatter_tokens(partial, rows):
    count, pair = lax.axis_size("seq"), lax.axis_size("head")
    low = partial.astype(bf16).reshape(count, pair, rows, partial.shape[1])
    low = lax.psum_scatter(low, "head", scatter_dimension=1, tiled=False)
    low = lax.psum_scatter(low, "seq", scatter_dimension=0, tiled=False)
    return low.astype(f32)


def cols_to_slices(weight):
    return lax.all_to_all(weight, "seq", split_axis=1, concat_axis=0, tiled=True)


def slices_to_cols(grad):
    return lax.all_to_all(grad, "seq", split_axis=0, concat_axis=1, tiled=True)


def member_groups(members):
    count = lax.axis_size("seq")
    return [[j * members + m for m in range(members)] for j in range(count // members)]


def chunked(array, width):
    return array.reshape((array.shape[0] // width, width) + array.shape[1:])


def split(array):
    high = array.astype(bf16)
    return high, (array - high.astype(f32)).astype(bf16)


def dot(left, right, dims):
    return lax.dot_general(left, right, (dims, ((), ())), preferred_element_type=f32)


NN = ((1,), (0,))
NT = ((1,), (1,))
TN = ((0,), (0,))


def dot2(left, right, dims):
    high, low = split(left)
    return dot(high, right, dims) + dot(low, right, dims)


def dot3(left, right, dims):
    lh, ll = split(left)
    rh, rl = split(right)
    return dot(lh, rh, dims) + (dot(lh, rl, dims) + dot(ll, rh, dims))


def unit_inverse(system, width):
    rows = lax.broadcasted_iota(jnp.int32, (width, width), 0)
    cols = lax.broadcasted_iota(jnp.int32, (width, width), 1)
    inverse = jnp.where(rows == cols, 1.0, 0.0)
    block = 1
    while block < width:
        mask = ((rows // block) % 2 == 1) & (cols // block == rows // block - 1)
        step = jnp.where(mask, system, 0.0)
        if block == 1:
            inverse = inverse - step
        else:
            inverse = inverse - dot3(dot3(inverse, step, NN), inverse, NN)
        block *= 2
    return inverse


CUM, RATE, BEGIN, FIRST = 0, 1, 2, 3


def chunk_masks(width, first):
    rows = lax.broadcasted_iota(jnp.int32, (width, width), 0)
    cols = lax.broadcasted_iota(jnp.int32, (width, width), 1)
    keep = (first <= cols.astype(f32)) & (rows >= cols)
    return keep, keep & (rows > cols)


def forward_kernel(
    group, q_ref, k_ref, v_ref, col_ref, row_ref, out_ref, inv_ref, invk_ref, state_ref, new_ref, carry
):
    @pl.when(pl.program_id(0) == 0)
    def _():
        carry[...] = jnp.zeros_like(carry)

    width = q_ref.shape[1]
    prepared = []
    for i in range(group):
        q, k, v = q_ref[i], k_ref[i], v_ref[i]
        cols, rows = col_ref[i], row_ref[i]
        cum, rate = cols[:, CUM : CUM + 1], cols[:, RATE : RATE + 1]
        begin, first = cols[:, BEGIN : BEGIN + 1], cols[:, FIRST : FIRST + 1]
        keep, strict = chunk_masks(width, first)
        fading = jnp.exp(jnp.where(keep, cum - rows[CUM : CUM + 1], -10000.0))
        key_key = dot(k, k, NT)
        inverse = unit_inverse(jnp.where(strict, rate * key_key * fading, 0.0), width)
        inv_ref[i] = inverse
        scaled = inverse * rows[RATE : RATE + 1]
        inv_v = dot2(scaled, v, NN)
        inv_k = dot2(scaled * rows[BEGIN : BEGIN + 1], k, NN)
        invk_ref[i] = inv_k
        attend = dot(q, k, NT) * fading
        token = lax.broadcasted_iota(jnp.int32, (width, 1), 0).astype(f32)
        last = jnp.exp(
            jnp.where(first[width - 1 :] <= token, cum[width - 1 :] - cum, -10000.0)
        )
        prepared.append((q, k, inv_v, inv_k, attend, begin, last))
    state = carry[...]
    for i in range(group):
        q, k, inv_v, inv_k, attend, begin, last = prepared[i]
        state_ref[i] = state
        new = inv_v - dot3(inv_k, state, NN)
        new_ref[i] = new
        high, low = split(state)
        out_ref[i] = begin * (dot(q, high, NN) + dot(q, low, NN)) + dot3(attend, new, NN)
        high, low = split(last * new)
        state = begin[width - 1 :] * state + (dot(k, high, TN) + dot(k, low, TN))
    carry[...] = state


def backward_kernel(
    group,
    grad_ref,
    q_ref,
    k_ref,
    v_ref,
    col_ref,
    row_ref,
    inv_ref,
    invk_ref,
    state_ref,
    new_ref,
    gq_ref,
    gk_ref,
    gv_ref,
    gcol_ref,
    grow_ref,
    carry,
):
    @pl.when(pl.program_id(0) == 0)
    def _():
        carry[...] = jnp.zeros_like(carry)

    width = q_ref.shape[1]
    prepared = []
    for i in range(group):
        q, k, grad = q_ref[i], k_ref[i], grad_ref[i]
        cols, rows = col_ref[i], row_ref[i]
        cum, rate = cols[:, CUM : CUM + 1], cols[:, RATE : RATE + 1]
        begin, first = cols[:, BEGIN : BEGIN + 1], cols[:, FIRST : FIRST + 1]
        keep, strict = chunk_masks(width, first)
        fading = jnp.exp(jnp.where(keep, cum - rows[CUM : CUM + 1], -10000.0))
        query_key = dot(q, k, NT)
        att_grad = dot3(query_key * fading, grad, TN)
        high, low = split(begin * grad)
        inv_k = invk_ref[i]
        base = (dot(q, high, TN) + dot(q, low, TN)) - dot3(inv_k, att_grad, TN)
        token = lax.broadcasted_iota(jnp.int32, (width, 1), 0).astype(f32)
        last = jnp.exp(
            jnp.where(first[width - 1 :] <= token, cum[width - 1 :] - cum, -10000.0)
        )
        prepared.append((q, k, grad, fading, strict, query_key, att_grad, base, rate, begin, last))
    pull = carry[...]
    chained = [None] * group
    for i in reversed(range(group)):
        q, k, grad, fading, strict, query_key, att_grad, base, rate, begin, last = prepared[i]
        high, low = split(pull)
        back = last * (dot(k, high, NN) + dot(k, low, NN))
        chained[i] = (pull, att_grad + back)
        pull = begin[width - 1 :] * pull + base - dot3(invk_ref[i], back, TN)
    carry[...] = pull
    lanes = lax.broadcasted_iota(jnp.int32, gcol_ref.shape[1:], 1)
    token = lax.broadcasted_iota(jnp.int32, (width, 1), 0)
    for i in range(group):
        q, k, grad, fading, strict, query_key, att_grad, base, rate, begin, last = prepared[i]
        pull, grad_new = chained[i]
        v, state, new = v_ref[i].astype(f32), state_ref[i], new_ref[i]
        grad_rhs = dot3(inv_ref[i], grad_new, TN)
        sh, sl = split(state)
        key_state = dot(k, sh, NN) + dot(k, sl, NN)
        query_state = dot(q, sh, NN) + dot(q, sl, NN)
        inside = v - begin * key_state
        grad_att = dot3(grad, new, NT)
        grad_system = jnp.where(strict, -dot3(grad_rhs, new, NT), 0.0)
        lower_fade = jnp.where(strict, dot(k, k, NT) * fading, 0.0)
        grad_rate = jnp.sum(grad_system * lower_fade, axis=1, keepdims=True) + jnp.sum(
            grad_rhs * inside, axis=1, keepdims=True
        )
        grad_lower = rate * grad_system
        grad_v = rate * grad_rhs
        gv_ref[i] = grad_v
        grad_begin = jnp.sum(grad * query_state - grad_v * key_state, axis=1, keepdims=True)
        qh, ql = split(fading * grad_att)
        kh, kl = split(fading * grad_lower)
        gq_ref[i] = begin * dot3(grad, state, NT) + (dot(qh, k, NN) + dot(ql, k, NN))
        pull_k = dot3(new, pull, NT)
        gk_ref[i] = (
            (dot(qh, q, TN) + dot(ql, q, TN))
            + (dot(kh, k, NN) + dot(kl, k, NN))
            + (dot(kh, k, TN) + dot(kl, k, TN))
            - begin * dot3(grad_v, state, NT)
            + last * pull_k
        )
        grad_last = jnp.sum(jnp.sum(pull * state, axis=1, keepdims=True), axis=0, keepdims=True)
        last_part = last * jnp.sum(pull_k * k.astype(f32), axis=1, keepdims=True)
        faded = grad_att * query_key * fading + grad_lower * lower_fade
        grad_cum = jnp.sum(faded, axis=1, keepdims=True) - last_part + grad_begin * begin
        at_end = jnp.sum(last_part, axis=0, keepdims=True) + grad_last * begin[width - 1 :]
        grad_cum = grad_cum + jnp.where(token == width - 1, at_end, 0.0)
        gcol_ref[i] = jnp.where(lanes == 0, grad_cum, jnp.where(lanes == 1, grad_rate, 0.0))
        grow_ref[i] = jnp.broadcast_to(jnp.sum(faded, axis=0, keepdims=True), grow_ref.shape[1:])


def blocks_of(group, array, order):
    tail = array.shape[1:]
    zeros = (0,) * len(tail)
    return pl.BlockSpec((group,) + tail, lambda i: (order(i),) + zeros)


def chunk_group(chunks):
    return 4 if chunks % 4 == 0 else 1


def shape_of(*dims):
    return jax.ShapeDtypeStruct(dims, f32)


def recurrence_forward(q, k, v, cols, rows):
    chunks, width, key_width = q.shape
    value = v.shape[2]
    group = chunk_group(chunks)
    outs = [
        shape_of(chunks, width, value),
        shape_of(chunks, width, width),
        shape_of(chunks, width, key_width),
        shape_of(chunks, key_width, value),
        shape_of(chunks, width, value),
    ]
    return pl.pallas_call(
        functools.partial(forward_kernel, group),
        grid=(chunks // group,),
        in_specs=[blocks_of(group, a, lambda i: i) for a in (q, k, v, cols, rows)],
        out_specs=[blocks_of(group, a, lambda i: i) for a in outs],
        out_shape=outs,
        scratch_shapes=[pltpu.VMEM((key_width, value), f32)],
        compiler_params=pltpu.CompilerParams(vmem_limit_bytes=48 * 2**20),
        name="delta_forward",
    )(q, k, v, cols, rows)


def recurrence_backward(grad, q, k, v, cols, rows, kept):
    chunks, width, key_width = q.shape
    value = v.shape[2]
    group = chunk_group(chunks)
    steps = chunks // group
    outs = [
        shape_of(chunks, width, key_width),
        shape_of(chunks, width, key_width),
        shape_of(chunks, width, value),
        shape_of(chunks, width, 8),
        shape_of(chunks, 8, width),
    ]
    args = (grad, q, k, v, cols, rows) + tuple(kept)
    return pl.pallas_call(
        functools.partial(backward_kernel, group),
        grid=(steps,),
        in_specs=[blocks_of(group, a, lambda i: steps - 1 - i) for a in args],
        out_specs=[blocks_of(group, a, lambda i: steps - 1 - i) for a in outs],
        out_shape=outs,
        scratch_shapes=[pltpu.VMEM((key_width, value), f32)],
        compiler_params=pltpu.CompilerParams(vmem_limit_bytes=48 * 2**20),
        name="delta_backward",
    )(*args)


def shifted(array, offset):
    if offset == 0:
        return array
    if offset > 0:
        return jnp.pad(array[:-offset], ((offset, 0), (0, 0)))
    return jnp.pad(array[-offset:], ((0, -offset), (0, 0)))


def filtered(pre, taps, valid):
    wide = pre.astype(f32)
    total = taps[0] * wide
    for offset in range(1, taps.shape[0]):
        total = total + taps[offset] * shifted(wide, offset) * valid[offset]
    return total


def filtered_back(grad, pre, taps, valid):
    wide = pre.astype(f32)
    total = taps[0] * grad
    grad_taps = [jnp.sum(grad * wide, axis=0)]
    for offset in range(1, taps.shape[0]):
        part = grad * valid[offset]
        total = total + taps[offset] * shifted(part, -offset)
        grad_taps.append(jnp.sum(part * shifted(wide, offset), axis=0))
    return total, jnp.stack(grad_taps)


def silu_back(grad, z):
    s = jax.nn.sigmoid(z)
    return grad * s * (1.0 + z * (1.0 - s))


def unit_back(grad, conv, inv, scale):
    inner = jnp.sum(grad * conv, axis=1, keepdims=True)
    return scale * (inv * grad - inv * inv * inv * inner * conv)


def norm_back(grad, values, inv, gain):
    normed = values * inv
    e = grad * gain
    return inv * (e - normed * jnp.mean(e * normed, axis=-1, keepdims=True)), jnp.sum(
        grad * normed, axis=0
    )


def on_device(
    stream_in,
    doc_start,
    first_gain,
    w_query,
    w_key,
    w_value,
    w_outgate,
    w_decay,
    w_rate,
    conv_query,
    conv_key,
    conv_value,
    a_log,
    dt_bias,
    out_gain,
    w_out,
    second_gain,
    w_gate,
    w_up,
    w_down,
    cotangent,
):
    count, pair = lax.axis_size("seq"), lax.axis_size("head")
    me, core_id = lax.axis_index("seq"), lax.axis_index("head")
    tok_rows, model = stream_in.shape
    heads = a_log.shape[0]
    members = count // heads
    head_id, member = me // members, me % members
    groups = member_groups(members)
    key_width = w_query.shape[1] // heads
    value_width = w_value.shape[1] // heads
    slice_width = value_width // members
    tokens = tok_rows * count
    rows = tok_rows // pair
    ff_slice = w_gate.shape[1] // count

    def own_rows(array):
        return lax.dynamic_slice_in_dim(array, core_id * rows, rows, 0)

    def pick(array, start, width, axis):
        return lax.dynamic_slice_in_dim(array, start, width, axis)

    s_query = lax.all_gather(
        cols_to_slices(w_query), "seq", axis=1, tiled=True, axis_index_groups=groups
    )
    s_key = lax.all_gather(
        cols_to_slices(w_key), "seq", axis=1, tiled=True, axis_index_groups=groups
    )
    s_value = cols_to_slices(w_value)
    s_outgate = cols_to_slices(w_outgate)
    thin = lax.all_gather(jnp.concatenate([w_decay, w_rate], axis=1), "seq", axis=0, tiled=True)
    s_decay = pick(thin, head_id, 1, 1)
    s_rate = pick(thin, heads + head_id, 1, 1)
    s_mixer = jnp.concatenate([s_query, s_key, s_value, s_outgate, s_decay, s_rate], axis=1)
    s_out = slices_to_cols(w_out)
    s_ffn = jnp.concatenate([cols_to_slices(w_gate), cols_to_slices(w_up)], axis=1)
    s_down = slices_to_cols(w_down)

    stream = own_rows(stream_in).astype(f32)
    inv_one = lax.rsqrt(jnp.mean(stream * stream, axis=-1, keepdims=True) + 1e-6)
    hidden_one = gather_tokens((stream * inv_one * first_gain).astype(bf16))
    cot_rows = own_rows(cotangent)
    cot_all = gather_tokens(cot_rows)
    starts = lax.all_gather(doc_start, "seq", axis=0, tiled=True)
    places = jnp.arange(tokens, dtype=jnp.int32)

    projected = mm(hidden_one, s_mixer)
    bounds = [0, key_width, 2 * key_width, 2 * key_width + slice_width]
    bounds.append(bounds[-1] + slice_width)
    pre_query = projected[:, bounds[0] : bounds[1]].astype(bf16)
    pre_key = projected[:, bounds[1] : bounds[2]].astype(bf16)
    pre_value = projected[:, bounds[2] : bounds[3]].astype(bf16)
    gate_value = projected[:, bounds[3] : bounds[4]]
    decay_raw = projected[:, bounds[4]]
    rate_raw = projected[:, bounds[4] + 1]

    taps_q = pick(conv_query, head_id * key_width, key_width, 1)
    taps_k = pick(conv_key, head_id * key_width, key_width, 1)
    taps_v = pick(conv_value, me * slice_width, slice_width, 1)
    valid = [
        (places - offset >= starts).astype(f32)[:, None] for offset in range(conv_query.shape[0])
    ]
    z_q = filtered(pre_query, taps_q, valid)
    z_k = filtered(pre_key, taps_k, valid)
    z_v = filtered(pre_value, taps_v, valid)
    c_q, c_k, c_v = jax.nn.silu(z_q), jax.nn.silu(z_k), jax.nn.silu(z_v)
    scale = key_width ** (-0.5)
    inv_q = lax.rsqrt(jnp.sum(c_q * c_q, axis=1, keepdims=True) + 1e-6)
    inv_k = lax.rsqrt(jnp.sum(c_k * c_k, axis=1, keepdims=True) + 1e-6)
    q = (c_q * inv_q * scale).astype(bf16)
    k = (c_k * inv_k).astype(bf16)
    v = c_v.astype(bf16)
    rate = jax.nn.sigmoid(rate_raw)
    own_a = -jnp.exp(pick(a_log, head_id, 1, 0))
    soft_in = decay_raw + pick(dt_bias, head_id, 1, 0)
    log_decay = own_a * jax.nn.softplus(soft_in)

    cut = tok_rows
    cum = jnp.cumsum(chunked(log_decay, cut), axis=1)
    chunk_begin = jnp.arange(0, tokens, cut, dtype=jnp.int32)[:, None]
    from_before = (chunked(starts, cut) < chunk_begin).astype(f32)
    first = jnp.maximum(chunked(starts, cut) - chunk_begin, 0).astype(f32)
    rows_in = jnp.stack([cum, chunked(rate, cut), jnp.exp(cum) * from_before, first], axis=1)
    rows_in = jnp.concatenate([rows_in, jnp.zeros_like(rows_in)], axis=1)
    cols_in = jnp.swapaxes(rows_in, 1, 2)
    chunks = [chunked(part, cut) for part in (q, k, v)] + [cols_in, rows_in]
    out, *kept = recurrence_forward(*chunks)
    core = out.reshape(tokens, slice_width)

    own_gain = pick(out_gain, member * slice_width, slice_width, 0)
    square = lax.psum(jnp.sum(core * core, axis=1), "seq", axis_index_groups=groups)
    inv_core = lax.rsqrt(square / value_width + 1e-5)[:, None]
    normed_core = core * inv_core
    silu_gate = jax.nn.silu(gate_value)
    gated = (normed_core * own_gain * silu_gate).astype(bf16)

    middle = stream + scatter_tokens(mm(gated, s_out), rows)
    inv_two = lax.rsqrt(jnp.mean(middle * middle, axis=-1, keepdims=True) + 1e-6)
    hidden_two = gather_tokens((middle * inv_two * second_gain).astype(bf16))

    gate_up = mm(hidden_two, s_ffn)
    gate_pre, up_pre = gate_up[:, :ff_slice], gate_up[:, ff_slice:]
    sig = jax.nn.sigmoid(gate_pre)
    silu_pre = gate_pre * sig
    inner = (silu_pre * up_pre).astype(bf16)
    ffn_out = scatter_tokens(mm(inner, s_down), rows)
    output = (middle + ffn_out).astype(bf16)
    grad_inner = mm_nt(cot_all, s_down)
    grad_gate_pre = (grad_inner * up_pre * sig * (1.0 + gate_pre * (1.0 - sig))).astype(bf16)
    grad_up_pre = (grad_inner * silu_pre).astype(bf16)
    grad_gate_up = jnp.concatenate([grad_gate_pre, grad_up_pre], axis=1)
    grad_two = scatter_tokens(mm_nt(grad_gate_up, s_ffn), rows)
    g_down = mm_tn(inner, cot_all)
    g_ffn = mm_tn(hidden_two, grad_gate_up)

    grad_back, grad_second = norm_back(grad_two, middle, inv_two, second_gain)
    grad_middle = cot_rows.astype(f32) + grad_back
    grad_mixer = gather_tokens(grad_middle.astype(bf16))
    g_out = mm_tn(gated, grad_mixer)
    grad_gated = mm_nt(grad_mixer, s_out)

    grad_scaled = grad_gated * silu_gate
    grad_out_gain = jnp.sum(grad_scaled * normed_core, axis=0)
    e = grad_scaled * own_gain
    dots = lax.psum(jnp.sum(e * normed_core, axis=1), "seq", axis_index_groups=groups)
    grad_core = inv_core * (e - normed_core * (dots / value_width)[:, None])
    grad_gate = silu_back(grad_gated * normed_core * own_gain, gate_value).astype(bf16)

    grad_q, grad_k, grad_v, grad_cols, grad_rows = recurrence_backward(
        chunked(grad_core, cut), *chunks, kept
    )
    grad_q = grad_q.reshape(tokens, key_width)
    grad_k = grad_k.reshape(tokens, key_width)
    grad_v = grad_v.reshape(tokens, slice_width)
    grad_cum = grad_cols[:, :, 0] - grad_rows[:, 0]
    grad_log = jnp.cumsum(grad_cum[:, ::-1], axis=1)[:, ::-1].reshape(-1)
    grad_rate_raw = grad_cols[:, :, 1].reshape(-1) * rate * (1.0 - rate)
    grad_a = jnp.sum(grad_log * log_decay)
    grad_decay_raw = grad_log * own_a * jax.nn.sigmoid(soft_in)
    grad_bias = jnp.sum(grad_decay_raw)

    grad_zq = silu_back(unit_back(grad_q, c_q, inv_q, scale), z_q)
    grad_zk = silu_back(unit_back(grad_k, c_k, inv_k, 1.0), z_k)
    grad_zv = silu_back(grad_v, z_v)
    gp_query, g_taps_q = filtered_back(grad_zq, pre_query, taps_q, valid)
    gp_key, g_taps_k = filtered_back(grad_zk, pre_key, taps_k, valid)
    gp_value, g_taps_v = filtered_back(grad_zv, pre_value, taps_v, valid)

    grad_proj = jnp.concatenate(
        [
            gp_query.astype(bf16),
            gp_key.astype(bf16),
            gp_value.astype(bf16),
            grad_gate,
            grad_decay_raw.astype(bf16)[:, None],
            grad_rate_raw.astype(bf16)[:, None],
        ],
        axis=1,
    )
    grad_one = scatter_tokens(mm_nt(grad_proj, s_mixer), rows)
    g_proj = mm_tn(hidden_one, grad_proj[:, : bounds[4]])
    grad_stream, grad_first = norm_back(grad_one, stream, inv_one, first_gain)
    grad_input = grad_middle + grad_stream

    def summed_slices(part):
        part = lax.psum_scatter(
            part.astype(bf16),
            "seq",
            scatter_dimension=1,
            tiled=True,
            axis_index_groups=groups,
        )
        return slices_to_cols(part).astype(f32)

    gw_query = summed_slices(g_proj[:, bounds[0] : bounds[1]])
    gw_key = summed_slices(g_proj[:, bounds[1] : bounds[2]])
    gw_value = slices_to_cols(g_proj[:, bounds[2] : bounds[3]].astype(bf16)).astype(f32)
    gw_outgate = slices_to_cols(g_proj[:, bounds[3] : bounds[4]].astype(bf16)).astype(f32)
    gw_out = cols_to_slices(g_out.astype(bf16)).astype(f32)
    gw_gate = slices_to_cols(g_ffn[:, :ff_slice].astype(bf16)).astype(f32)
    gw_up = slices_to_cols(g_ffn[:, ff_slice:].astype(bf16)).astype(f32)
    gw_down = cols_to_slices(g_down.astype(bf16)).astype(f32)

    thin_grads = lax.all_gather(jnp.stack([grad_decay_raw, grad_rate_raw]), "seq")
    thin_grads = jnp.sum(thin_grads.reshape(heads, members, 2, tokens), axis=1)
    own_cols = pick(hidden_one, me * w_decay.shape[0], w_decay.shape[0], 1).astype(f32)
    thin_grads = jnp.einsum("td,hgt->gdh", own_cols, thin_grads, precision=highest)

    def placed(part, start, width, axis):
        shape = list(part.shape)
        shape[axis] = width
        return lax.dynamic_update_slice_in_dim(jnp.zeros(shape, f32), part, start, axis)

    small = lax.psum(
        (
            placed(g_taps_q, head_id * key_width, conv_query.shape[1], 1),
            placed(g_taps_k, head_id * key_width, conv_key.shape[1], 1),
            placed(g_taps_v, me * slice_width, conv_value.shape[1], 1),
            placed(grad_a[None], head_id, heads, 0),
            placed(grad_bias[None], head_id, heads, 0),
        ),
        "seq",
    )
    gains = lax.psum(
        (
            grad_first,
            grad_second,
            placed(grad_out_gain, member * slice_width, value_width, 0),
        ),
        ("seq", "head"),
    )
    return (
        lax.all_gather(output, "head", axis=0, tiled=True),
        lax.all_gather(grad_input, "head", axis=0, tiled=True),
        gains[0],
        gw_query,
        gw_key,
        gw_value,
        gw_outgate,
        thin_grads[0],
        thin_grads[1],
        small[0],
        small[1],
        small[2],
        small[3],
        small[4],
        gains[2],
        gw_out,
        gains[1],
        gw_gate,
        gw_up,
        gw_down,
    )


def solution(mesh):
    in_specs = (
        P("seq", None),
        P("seq"),
        P(),
        P("seq", "head"),
        P("seq", "head"),
        P("seq", "head"),
        P("seq", "head"),
        P("seq", "head"),
        P("seq", "head"),
        P(None, "head"),
        P(None, "head"),
        P(None, "head"),
        P("head"),
        P("head"),
        P(),
        P("head", "seq"),
        P(),
        P("seq", "head"),
        P("seq", "head"),
        P("head", "seq"),
        P("seq", None),
    )
    out_specs = (
        P("seq", None),
        P("seq", None),
        P(),
        P("seq", "head"),
        P("seq", "head"),
        P("seq", "head"),
        P("seq", "head"),
        P("seq", "head"),
        P("seq", "head"),
        P(None, "head"),
        P(None, "head"),
        P(None, "head"),
        P("head"),
        P("head"),
        P(),
        P("head", "seq"),
        P(),
        P("seq", "head"),
        P("seq", "head"),
        P("head", "seq"),
    )
    return jax.shard_map(
        on_device, mesh=mesh, in_specs=in_specs, out_specs=out_specs, check_vma=False
    )
```

```python
import functools

import jax
import jax.numpy as jnp
from jax import lax
from jax.experimental import pallas as pl
from jax.experimental.pallas import tpu as pltpu
from jax.sharding import PartitionSpec as P

bf16 = jnp.bfloat16
f32 = jnp.float32
LANES = 128
VMEM_LIMIT = 56 * 2**20


def mm(left, right):
    return jnp.dot(left, right, preferred_element_type=f32)


def mm_nt(left, right):
    return lax.dot_general(left, right, (((1,), (1,)), ((), ())), preferred_element_type=f32)


def mm_tn(left, right):
    return lax.dot_general(left, right, (((0,), (0,)), ((), ())), preferred_element_type=f32)


def near(count):
    return count == 16


def across(value, offset):
    count = lax.axis_size("seq")
    return lax.ppermute(value, "seq", [(i, i ^ offset) for i in range(count)])


def other_core(value):
    return lax.ppermute(value, "head", [(0, 1), (1, 0)])


def after(value, *others):
    return lax.optimization_barrier((value, others))[0]


ALL, PAIR = (1, 2, 3), (2,)


def block_places():
    count = lax.axis_size("seq")
    blocks = jnp.arange(count, dtype=jnp.int32)
    if not near(count):
        return jnp.concatenate([blocks, jnp.zeros((1,), jnp.int32)])
    apart = blocks ^ lax.axis_index("seq")
    flip = lax.axis_index("head").astype(jnp.int32)
    return jnp.concatenate([(apart % 4) * 4 + apart // 4, flip[None]])


def exchanged(blocks):
    groups = [[4 * z + j for j in range(4)] for z in range(4)]
    return lax.all_to_all(
        blocks, "seq", split_axis=0, concat_axis=0, tiled=True, axis_index_groups=groups
    )


def to_all(value):
    return jnp.broadcast_to(value[None], (4,) + value.shape)


def gather_z(rows, zs=ALL):
    if not near(lax.axis_size("seq")):
        return [rows]
    own = rows[None]
    moved = [across(own, 4 * z) for z in zs], across(own, 1), across(own, 2)
    along_z, x_first, y_first = after(moved)
    return own, along_z, x_first, y_first


def gather_xy(state):
    if not near(lax.axis_size("seq")):
        return state
    own, along_z, x_first, y_first = state
    rest = jnp.concatenate(along_z, axis=0)
    x_rest, y_rest, corner = after((across(rest, 1), across(rest, 2), across(y_first, 1)))
    return own, rest, x_first, x_rest, y_first, y_rest, corner


def gather_corner(sides):
    if not near(lax.axis_size("seq")):
        return sides
    half = sides[1].shape[0] // 2
    x_rest, y_rest = sides[3], sides[5]
    corner = [across(y_rest[:half], 1)] if half else []
    return list(sides) + corner + [across(x_rest[half:], 2)]


def gather_end(parts):
    if not near(lax.axis_size("seq")):
        out = lax.all_gather(lax.all_gather(parts[0], "seq"), "head")
        return out[0], out[1]
    mine = jnp.concatenate(parts, axis=0)
    return mine, other_core(mine)


def scatter_begin(left, right, dims):
    blocks, rows = left[0].shape[:2]
    mine, theirs = (part.reshape(blocks * rows, -1) for part in left)

    def product(part):
        return lax.dot_general(part, right, (dims, ((), ())), preferred_element_type=f32)

    if not near(lax.axis_size("seq")):
        low = jnp.stack([product(mine), product(theirs)]).astype(bf16)
        low = lax.psum_scatter(low.reshape(2, blocks, rows, -1), "head", scatter_dimension=0)
        return low, low
    size = blocks // 2 * rows
    sent = [product(theirs[size * half : size * (half + 1)]).astype(bf16) for half in (0, 1)]
    total = [None, None]
    for half in (1, 0):
        part = product(mine[size * half : size * (half + 1)])
        total[half] = part + other_core(sent[half]).astype(f32)
    half, quarter = size // 2, size // 4
    groups = [total[group // 2][(group % 2) * half :][:half] for group in range(4)]
    return [[part[:quarter], part[quarter:]] for part in groups], sent[0]


def scatter_corner(halves, hold=()):
    if not near(lax.axis_size("seq")):
        return halves, halves
    low = [part.astype(bf16) for part in halves[3]]
    if hold:
        low[0] = after(low[0], *hold)
    mid = low[0].shape[1] // 2
    moved = [None, None]
    for half in (1, 0):
        moved[half] = across(low[half][:, :mid], 1), across(low[half][:, mid:], 2)
    return (halves, moved), low[0]


def scatter_xy(state):
    if not near(lax.axis_size("seq")):
        return state, state
    halves, moved = state
    columns = [None, None]
    for half in (1, 0):
        by_x, by_y = (part.astype(f32) for part in moved[half])
        mid = by_x.shape[1]
        y_part = halves[2][half] + jnp.pad(by_x, ((0, 0), (0, mid)))
        x_part = halves[1][half] + jnp.pad(by_y, ((0, 0), (mid, 0)))
        x_low, y_low = x_part.astype(bf16), y_part.astype(bf16)
        columns[half] = halves[0][half], across(x_low, 1), across(y_low, 2)
    return columns, y_low


def scatter_z(columns, rows, zs=ALL):
    if not near(lax.axis_size("seq")):
        return lax.psum_scatter(columns, "seq", scatter_dimension=0).astype(f32), columns
    summed = [base + x.astype(f32) + y.astype(f32) for base, x, y in columns]
    parts = [part[at : at + rows] for part in summed for at in range(0, part.shape[0], rows)]
    total = parts[0]
    for part, z in reversed(list(zip(parts[1:], zs))):
        low = part.astype(bf16)
        total = total + across(low, 4 * z).astype(f32)
    return total, low


def neighbour_slices(part, axis, cuts):
    if not near(lax.axis_size("seq")):
        return [None] * cuts
    return [across(piece, 4) for piece in jnp.split(part, cuts, axis=axis)]


def with_slices(part, pieces, axis):
    if pieces[0] is None:
        return part
    return jnp.concatenate([part] + pieces, axis=axis)


def neighbour_parts(part, axis, cuts):
    if not near(lax.axis_size("seq")):
        return part, []
    size = part.shape[axis] // 2
    mine, theirs = (lax.slice_in_dim(part, at, at + size, axis=axis) for at in (0, size))
    pieces = jnp.split(theirs.astype(bf16), cuts, axis=axis)
    return mine, [across(piece, 4) for piece in pieces]


def add_parts(mine, pieces, axis):
    if not pieces:
        return mine
    return mine + jnp.concatenate([piece.astype(f32) for piece in pieces], axis=axis)


def as_tiles(array, count):
    rows = array.shape[0] // count
    tiles = array.reshape(count, rows, -1, LANES)
    return jnp.swapaxes(tiles, 1, 2).reshape(count, -1, LANES)


def from_tiles(tiles, rows):
    count = tiles.shape[0]
    tiles = tiles.reshape(count, -1, rows, LANES)
    return jnp.swapaxes(tiles, 1, 2).reshape(count, rows, -1)


def all_to_all(blocks):
    return lax.all_to_all(blocks, "seq", split_axis=0, concat_axis=0, tiled=True)


def in_order(parts, place):
    count = parts[0].shape[0]
    return tuple(jnp.take(part, place[:count], axis=0) for part in parts)


def stream_order(parts, place):
    count, rows = parts[0].shape[:2]
    mine, theirs = in_order(parts, place)
    straight = place[count] == 0
    low, high = jnp.where(straight, mine, theirs), jnp.where(straight, theirs, mine)
    return jnp.concatenate([low, high], axis=1)


def both_halves(rows):
    theirs = other_core(rows)
    first = lax.axis_index("head") == 0
    return jnp.concatenate([jnp.where(first, rows, theirs), jnp.where(first, theirs, rows)], axis=0)


def sum_members(value, members):
    count = lax.axis_size("seq")
    if not near(count):
        groups = [[j * members + m for m in range(members)] for j in range(count // members)]
        return lax.psum(value, "seq", axis_index_groups=groups)
    return value + across(value, 1) + across(value, 2) + across(value, 3)


def sum_stream(value):
    count = lax.axis_size("seq")
    if not near(count):
        return lax.psum(value, "seq")
    for offset in (1, 2, 4, 8):
        value = value + across(value, offset)
    return value


def to_slices(blocks):
    out = lax.all_to_all(blocks, "seq", split_axis=1, concat_axis=0, tiled=True)
    return out.reshape((-1, blocks.shape[2]))


def from_slices(grad, rows):
    blocks = grad.reshape((-1, rows, grad.shape[1]))
    return lax.all_to_all(blocks, "seq", split_axis=0, concat_axis=0, tiled=True)


def widened(array, width, axis):
    pads = [(0, 0)] * array.ndim
    pads[axis] = (0, width - array.shape[axis])
    return jnp.pad(array, pads)


def split(array):
    high = array.astype(bf16)
    return high, (array - high.astype(f32)).astype(bf16)


def dot(left, right, dims):
    return lax.dot_general(left, right, (dims, ((), ())), preferred_element_type=f32)


NN = ((1,), (0,))
NT = ((1,), (1,))
TN = ((0,), (0,))


def dot2(left, right, dims):
    high, low = split(left)
    return dot(high, right, dims) + dot(low, right, dims)


def dot3(left, right, dims):
    lh, ll = split(left)
    rh, rl = split(right)
    return dot(lh, rh, dims) + (dot(lh, rl, dims) + dot(ll, rh, dims))


def exact_sum(selector, array):
    high, low = split(array)
    rest = (array - high.astype(f32) - low.astype(f32)).astype(bf16)
    return dot(selector, high, NN) + dot(selector, low, NN) + dot(selector, rest, NN)


def square_iota(width):
    rows = lax.broadcasted_iota(jnp.int32, (width, width), 0)
    return rows, lax.broadcasted_iota(jnp.int32, (width, width), 1)


def unit_inverses(systems, width):
    rows, cols = square_iota(width)
    inverses = [jnp.where(rows == cols, 1.0, 0.0)] * len(systems)
    block = 1
    while block < width:
        mask = ((rows // block) % 2 == 1) & (cols // block == rows // block - 1)
        steps = [jnp.where(mask, system, 0.0) for system in systems]
        if block > 1:
            steps = [dot3(inverse, step, NN) for inverse, step in zip(inverses, steps)]
            steps = [dot3(step, inverse, NN) for inverse, step in zip(inverses, steps)]
        inverses = [inverse - step for inverse, step in zip(inverses, steps)]
        block *= 2
    return inverses


def in_lanes(width, *columns):
    lanes = lax.broadcasted_iota(jnp.int32, (width, LANES), 1)
    out = jnp.zeros((width, LANES), f32)
    for place, column in enumerate(columns):
        out = jnp.where(lanes == place, column, out)
    return out


def lane(array, place):
    return array[:, place : place + 1]


def as_column(row):
    return lane(jnp.broadcast_to(row, (LANES, LANES)).T, 0)


CUM, RATE, BEGIN, LOG, SOFT = 0, 1, 2, 3, 4


def chunk_masks(width, first):
    rows, cols = square_iota(width)
    keep = (first <= cols.astype(f32)) & (rows >= cols)
    return keep, keep & (rows > cols)


def fade(width, cols, rows, start):
    first = jnp.maximum(start, 0.0)
    keep, strict = chunk_masks(width, first)
    cum = lane(cols, CUM)
    fading = jnp.exp(jnp.where(keep, cum - rows[CUM : CUM + 1], -10000.0))
    token = lax.broadcasted_iota(jnp.int32, (width, 1), 0).astype(f32)
    last = jnp.exp(jnp.where(first[width - 1 :] <= token, cum[width - 1 :] - cum, -10000.0))
    return fading, strict, last


def halves_of(low, high, flip):
    return jnp.where(flip == 0, low, high), jnp.where(flip == 0, high, low)


def whole_chunk(mine_ref, theirs_ref, place, flip):
    return jnp.concatenate(halves_of(mine_ref[place], theirs_ref[place], flip), axis=0)


def silu_back(grad, z):
    s = jax.nn.sigmoid(z)
    return grad * s * (1.0 + z * (1.0 - s))


def forward_kernel(group, key_width, place_ref, *refs):
    mine_refs, theirs_refs, refs = refs[:group], refs[group : 2 * group], refs[2 * group :]
    (start_ref, taps_ref, head_ref, core_ref, square_ref, z_ref, q_ref, k_ref, v_ref, col_ref) = refs[:10]
    inv_ref, invk_ref, state_ref, new_ref, carry, ext = refs[10:]
    step = pl.program_id(0)
    width = core_ref.shape[1]
    wide = z_ref.shape[2]
    flip = place_ref[place_ref.shape[0] - 1]

    @pl.when(step == 0)
    def _():
        carry[...] = jnp.zeros_like(carry)
        ext[...] = jnp.zeros_like(ext)

    ext[0, 0:8] = ext[group - 1, width : width + 8]
    token = lax.broadcasted_iota(jnp.int32, (width, 1), 0).astype(f32)
    rows_id, cols_id = square_iota(width)
    triangle = jnp.where(rows_id >= cols_id, 1.0, 0.0).astype(bf16)
    own_a, bias = head_ref[0:1, 0:1], head_ref[0:1, 1:2]
    prepared = []
    for i in range(group):
        x = whole_chunk(mine_refs[i], theirs_refs[i], 0, flip)
        pre = x[:, :wide].astype(bf16).astype(f32)
        ext[i, 8 : 8 + width] = pre
        if i + 1 < group:
            ext[i + 1, 0:8] = pre[width - 8 :]
        start = start_ref[i][:, 0:1]
        z = taps_ref[0:1] * pre
        for offset in range(1, 4):
            valid = jnp.where(token - offset >= start, 1.0, 0.0)
            z = z + taps_ref[offset : offset + 1] * ext[i, 8 - offset : 8 - offset + width] * valid
        z_ref[i] = z
        conv = z * jax.nn.sigmoid(z)
        cq, ck = conv[:, :key_width], conv[:, key_width : 2 * key_width]
        q = cq * lax.rsqrt(jnp.sum(cq * cq, axis=1, keepdims=True) + 1e-6) * key_width ** (-0.5)
        k = ck * lax.rsqrt(jnp.sum(ck * ck, axis=1, keepdims=True) + 1e-6)
        q, k, v = q.astype(bf16), k.astype(bf16), conv[:, 2 * key_width :].astype(bf16)
        q_ref[i], k_ref[i], v_ref[i] = q, k, v
        soft = lane(x, x.shape[1] - LANES) + bias
        rate = jax.nn.sigmoid(lane(x, x.shape[1] - LANES + 1))
        log_decay = own_a * (jnp.maximum(soft, 0.0) + jnp.log1p(jnp.exp(-jnp.abs(soft))))
        cum = lane(exact_sum(triangle, in_lanes(width, log_decay)), 0)
        begin = jnp.where(start < 0.0, jnp.exp(cum), 0.0)
        cols = in_lanes(width, cum, rate, begin, log_decay, soft)
        col_ref[i] = cols
        rows = cols.T
        fading, strict, last = fade(width, cols, rows, start)
        system = jnp.where(strict, rate * dot(k, k, NT) * fading, 0.0)
        attend = dot(q, k, NT) * fading
        prepared.append((q, k, v, rows, system, attend, begin, last))
    inverses = unit_inverses([part[4] for part in prepared], width)
    solved = []
    for i in range(group):
        q, k, v, rows = prepared[i][:4]
        inv_ref[i] = inverses[i]
        scaled = inverses[i] * rows[RATE : RATE + 1]
        inv_v = dot2(scaled, v, NN)
        inv_k = dot2(scaled * rows[BEGIN : BEGIN + 1], k, NN)
        invk_ref[i] = inv_k
        solved.append((inv_v, inv_k))
    state = carry[...]
    for i in range(group):
        q, k, _, _, _, attend, begin, last = prepared[i]
        inv_v, inv_k = solved[i]
        state_ref[i] = state
        new = inv_v - dot3(inv_k, state, NN)
        new_ref[i] = new
        high, low = split(state)
        core = begin * (dot(q, high, NN) + dot(q, low, NN)) + dot3(attend, new, NN)
        core_ref[i] = core
        squares = jnp.sum(core * core, axis=1, keepdims=True)
        square_ref[pl.ds(step * group + i, 1)] = in_lanes(width, squares).T[0:1]
        high, low = split(last * new)
        state = begin[width - 1 :] * state + (dot(k, high, TN) + dot(k, low, TN))
    carry[...] = state


def gate_kernel(place_ref, core_ref, mine_ref, theirs_ref, inv_ref, gain_ref, out_mine, out_theirs):
    count, width, _ = core_ref.shape
    half = width // 2
    flip = place_ref[count]

    def step(i, _):
        place = place_ref[i]
        inv = as_column(inv_ref[pl.ds(i, 1)])
        gate = whole_chunk(mine_ref, theirs_ref, place, flip)
        gated = core_ref[i] * inv * gain_ref[0:1] * (gate * jax.nn.sigmoid(gate))
        mine, theirs = halves_of(gated[:half], gated[half:], flip)
        out_mine[place] = mine.astype(bf16)
        out_theirs[place] = theirs.astype(bf16)
        return 0

    lax.fori_loop(0, count, step, 0, unroll=4)


def dots_kernel(
    place_ref, grad_mine, grad_theirs, core_ref, mine_ref, theirs_ref, inv_ref, gain_ref, out_ref
):
    count, width, _ = core_ref.shape
    flip = place_ref[count]

    def step(i, _):
        place = place_ref[i]
        inv = as_column(inv_ref[pl.ds(i, 1)])
        gate = whole_chunk(mine_ref, theirs_ref, place, flip)
        grad = whole_chunk(grad_mine, grad_theirs, place, flip)
        e = grad * (gate * jax.nn.sigmoid(gate)) * gain_ref[0:1]
        dots = jnp.sum(e * core_ref[i] * inv, axis=1, keepdims=True)
        out_ref[pl.ds(i, 1)] = in_lanes(width, dots).T[0:1]
        return 0

    lax.fori_loop(0, count, step, 0, unroll=4)


def backward_kernel(group, key_width, value_width, place_ref, *refs):
    placed, refs = refs[: 4 * group], refs[4 * group :]
    mine_refs, theirs_refs = placed[:group], placed[group : 2 * group]
    grad_mine, grad_theirs = placed[2 * group : 3 * group], placed[3 * group :]
    start_ref, taps_ref, head_ref, gain_ref, inv_core_ref, dots_ref = refs[:6]
    core_ref, z_ref, q_ref, k_ref, v_ref, col_ref, inv_ref, invk_ref, state_ref, new_ref = refs[6:16]
    out_mine, out_theirs, sum_ref, thin_ref, carry, ext = refs[16:]
    step = pl.program_id(0)
    width = core_ref.shape[1]
    half = width // 2
    wide = z_ref.shape[2]
    chunks = place_ref.shape[0] - 1
    flip = place_ref[chunks]
    base_chunk = chunks - group * (step + 1)

    @pl.when(step == 0)
    def _():
        carry[...] = jnp.zeros_like(carry)
        ext[...] = jnp.zeros_like(ext)
        sum_ref[...] = jnp.zeros_like(sum_ref)

    for offset in range(3):
        ext[offset, group - 1, width : width + 8] = ext[offset, 0, 0:8]
    own_a = head_ref[0:1, 0:1]
    gain = gain_ref[0:1]
    token = lax.broadcasted_iota(jnp.int32, (width, 1), 0).astype(f32)
    rows_id, cols_id = square_iota(width)
    triangle = jnp.where(rows_id <= cols_id, 1.0, 0.0).astype(bf16)
    every = range(group)
    xs = [whole_chunk(mine_refs[i], theirs_refs[i], 0, flip) for i in every]
    qs, ks = [q_ref[i] for i in every], [k_ref[i] for i in every]
    cols = [col_ref[i] for i in every]
    starts = [start_ref[i][:, 0:1] for i in every]
    rates, begins = [lane(c, RATE) for c in cols], [lane(c, BEGIN) for c in cols]
    fades = [fade(width, cols[i], cols[i].T, starts[i]) for i in every]
    query_key = [dot(qs[i], ks[i], NT) for i in every]
    grads, grad_gates = [], []
    for i in every:
        gate = xs[i][:, wide : wide + LANES]
        grad_gated = whole_chunk(grad_mine[i], grad_theirs[i], 0, flip)
        inv = as_column(inv_core_ref[pl.ds(base_chunk + i, 1)])
        dots = as_column(dots_ref[pl.ds(base_chunk + i, 1)])
        normed = core_ref[i] * inv
        sig = jax.nn.sigmoid(gate)
        scaled = grad_gated * (gate * sig)
        sum_ref[4:5, :LANES] += jnp.sum(scaled * normed, axis=0, keepdims=True)
        grads.append(inv * (scaled * gain - normed * (dots * (1.0 / value_width))))
        grad_gates.append(grad_gated * normed * gain * sig * (1.0 + gate * (1.0 - sig)))
    att_grads = [dot3(query_key[i] * fades[i][0], grads[i], TN) for i in every]
    bases = []
    for i in every:
        high, low = split(begins[i] * grads[i])
        bases.append((dot(qs[i], high, TN) + dot(qs[i], low, TN)) - dot3(invk_ref[i], att_grads[i], TN))
    pull = carry[...]
    pulls, grad_news = [None] * group, [None] * group
    for i in reversed(every):
        high, low = split(pull)
        back = fades[i][2] * (dot(ks[i], high, NN) + dot(ks[i], low, NN))
        pulls[i], grad_news[i] = pull, att_grads[i] + back
        pull = begins[i][width - 1 :] * pull + bases[i] - dot3(invk_ref[i], back, TN)
    carry[...] = pull
    grad_rhs = [dot3(inv_ref[i], grad_news[i], TN) for i in every]
    grad_atts = [dot3(grads[i], new_ref[i], NT) for i in every]
    lower_fades = [jnp.where(fades[i][1], dot(ks[i], ks[i], NT) * fades[i][0], 0.0) for i in every]
    key_states, query_states = [], []
    for i in every:
        high, low = split(state_ref[i])
        key_states.append(dot(ks[i], high, NN) + dot(ks[i], low, NN))
        query_states.append(dot(qs[i], high, NN) + dot(qs[i], low, NN))
    pull_ks = [dot3(new_ref[i], pulls[i], NT) for i in every]
    systems = [jnp.where(fades[i][1], -dot3(grad_rhs[i], new_ref[i], NT), 0.0) for i in every]
    grad_vs = [rates[i] * grad_rhs[i] for i in every]
    grad_qs, grad_ks = [], []
    for i in every:
        q, k, begin, last = qs[i], ks[i], begins[i], fades[i][2]
        qh, ql = split(fades[i][0] * grad_atts[i])
        kh, kl = split(fades[i][0] * rates[i] * systems[i])
        grad_qs.append(begin * dot3(grads[i], state_ref[i], NT) + (dot(qh, k, NN) + dot(ql, k, NN)))
        grad_ks.append(
            (dot(qh, q, TN) + dot(ql, q, TN))
            + (dot(kh, k, NN) + dot(kl, k, NN))
            + (dot(kh, k, TN) + dot(kl, k, TN))
            - begin * dot3(grad_vs[i], state_ref[i], NT)
            + last * pull_ks[i]
        )
    thins = []
    for i in every:
        rate, begin, last = rates[i], begins[i], fades[i][2]
        inside = v_ref[i].astype(f32) - begin * key_states[i]
        grad_rate = jnp.sum(systems[i] * lower_fades[i], axis=1, keepdims=True) + jnp.sum(
            grad_rhs[i] * inside, axis=1, keepdims=True
        )
        grad_begin = jnp.sum(
            grads[i] * query_states[i] - grad_vs[i] * key_states[i], axis=1, keepdims=True
        )
        grad_last = jnp.sum(
            jnp.sum(pulls[i] * state_ref[i], axis=1, keepdims=True), axis=0, keepdims=True
        )
        last_part = last * jnp.sum(pull_ks[i] * ks[i].astype(f32), axis=1, keepdims=True)
        faded = grad_atts[i] * query_key[i] * fades[i][0] + rate * systems[i] * lower_fades[i]
        grad_cum = (
            jnp.sum(faded, axis=1, keepdims=True)
            - as_column(jnp.sum(faded, axis=0, keepdims=True))
            - last_part
            + grad_begin * begin
        )
        at_end = jnp.sum(last_part, axis=0, keepdims=True) + grad_last * begin[width - 1 :]
        grad_cum = grad_cum + jnp.where(token == width - 1, at_end, 0.0)
        grad_log = lane(exact_sum(triangle, in_lanes(width, grad_cum)), 0)
        log_decay, soft = lane(cols[i], LOG), lane(cols[i], SOFT)
        grad_decay = grad_log * own_a * jax.nn.sigmoid(soft)
        thin = in_lanes(width, grad_decay, grad_rate * rate * (1.0 - rate))
        thin_ref[pl.ds(base_chunk + i, 1)] = thin.T[None, 0:8]
        sum_ref[5:6, :LANES] += jnp.sum(
            in_lanes(width, grad_log * log_decay, grad_decay), axis=0, keepdims=True
        )
        thins.append(thin)
    for i in reversed(every):
        z = z_ref[i]
        sig = jax.nn.sigmoid(z)
        conv = z * sig
        cq, ck = conv[:, :key_width], conv[:, key_width : 2 * key_width]
        iq = lax.rsqrt(jnp.sum(cq * cq, axis=1, keepdims=True) + 1e-6)
        ik = lax.rsqrt(jnp.sum(ck * ck, axis=1, keepdims=True) + 1e-6)
        dq = jnp.sum(grad_qs[i] * cq, axis=1, keepdims=True)
        dk = jnp.sum(grad_ks[i] * ck, axis=1, keepdims=True)
        scale = key_width ** (-0.5)
        grad_cq = (scale * iq) * (grad_qs[i] - (iq * iq * dq) * cq)
        grad_ck = ik * (grad_ks[i] - (ik * ik * dk) * ck)
        grad_z = jnp.concatenate([grad_cq, grad_ck, grad_vs[i]], axis=1)
        grad_z = grad_z * sig * (1.0 + z * (1.0 - sig))
        pre = xs[i][:, :wide].astype(bf16).astype(f32)
        grad_pre = taps_ref[0:1] * grad_z
        sum_ref[0:1] += jnp.sum(pre * grad_z, axis=0, keepdims=True)
        for offset in range(1, 4):
            valid = jnp.where(token - offset >= starts[i], 1.0, 0.0)
            part = grad_z * valid
            ext[offset - 1, i, 0:width] = part
            if i > 0:
                ext[offset - 1, i - 1, width : width + 8] = part[0:8]
            moved = ext[offset - 1, i, offset : offset + width]
            grad_pre = grad_pre + taps_ref[offset : offset + 1] * moved
            sum_ref[offset : offset + 1] += jnp.sum(pre * moved, axis=0, keepdims=True)
        out = jnp.concatenate([grad_pre, grad_gates[i], thins[i]], axis=1)
        place = place_ref[base_chunk + i]
        mine, theirs = halves_of(out[:half], out[half:], flip)
        out_mine[place] = mine.astype(bf16)
        out_theirs[place] = theirs.astype(bf16)


def stepped(group, array, order):
    tail = array.shape[1:]
    zeros = (0,) * len(tail)
    return pl.BlockSpec((group,) + tail, lambda i, place: (order(i),) + zeros)


def resident(array):
    zeros = (0,) * len(array.shape)
    return pl.BlockSpec(array.shape, lambda i, place: zeros)


def placed_blocks(group, array, order):
    def spec(c):
        shape = (1,) + array.shape[1:]
        return pl.BlockSpec(shape, lambda i, place: (place[group * order(i) + c], 0, 0))

    return [spec(c) for c in range(group)]


def chunk_group(chunks, most):
    return most if chunks % most == 0 else 1


def shape_of(*dims, dtype=f32):
    return jax.ShapeDtypeStruct(dims, dtype)


def cost(microseconds):
    return pl.CostEstimate(flops=0, bytes_accessed=int(microseconds * 3.6e6), transcendentals=0)


def params():
    return pltpu.CompilerParams(vmem_limit_bytes=VMEM_LIMIT)


def recurrence_forward(place, proj, start, taps, head, key_width):
    mine, theirs = proj
    chunks, width, wide = mine.shape[0], 2 * mine.shape[1], taps.shape[1]
    value = wide - 2 * key_width
    group = chunk_group(chunks, 8)
    outs = [
        shape_of(chunks, width, value),
        shape_of(chunks, width),
        shape_of(chunks, width, wide),
        shape_of(chunks, width, key_width, dtype=bf16),
        shape_of(chunks, width, key_width, dtype=bf16),
        shape_of(chunks, width, value, dtype=bf16),
        shape_of(chunks, width, LANES),
        shape_of(chunks, width, width),
        shape_of(chunks, width, key_width),
        shape_of(chunks, key_width, value),
        shape_of(chunks, width, value),
    ]
    order = lambda i: i
    out_specs = [stepped(group, a, order) for a in outs]
    out_specs[1] = resident(outs[1])
    return pl.pallas_call(
        functools.partial(forward_kernel, group, key_width),
        grid_spec=pltpu.PrefetchScalarGridSpec(
            num_scalar_prefetch=1,
            grid=(chunks // group,),
            in_specs=placed_blocks(group, mine, order)
            + placed_blocks(group, theirs, order)
            + [stepped(group, start, order), resident(taps), resident(head)],
            out_specs=out_specs,
            scratch_shapes=[
                pltpu.VMEM((key_width, value), f32),
                pltpu.VMEM((group, width + 8, wide), f32),
            ],
        ),
        out_shape=outs,
        compiler_params=params(),
        cost_estimate=cost(28.0 * chunks / 16),
        name="delta_forward",
    )(place, *([mine] * group), *([theirs] * group), start, taps, head)


def gate_spec(proj, wide):
    shape = proj.shape[:2] + (LANES,)
    return pl.BlockSpec(shape, lambda i, place: (0, 0, wide // LANES))


def gate_forward(place, core, proj, inv, gain, wide):
    mine, theirs = proj
    out = shape_of(*mine.shape[:2], LANES, dtype=bf16)
    return pl.pallas_call(
        gate_kernel,
        grid_spec=pltpu.PrefetchScalarGridSpec(
            num_scalar_prefetch=1,
            grid=(1,),
            in_specs=[
                resident(core),
                gate_spec(mine, wide),
                gate_spec(theirs, wide),
                resident(inv),
                resident(gain),
            ],
            out_specs=[resident(out), resident(out)],
        ),
        out_shape=[out, out],
        compiler_params=params(),
        cost_estimate=cost(4.0),
        name="gate_forward",
    )(place, core, mine, theirs, inv, gain)


def gate_dots(place, grad, core, proj, inv, gain, wide):
    mine, theirs = proj
    out = shape_of(*core.shape[:2])
    return pl.pallas_call(
        dots_kernel,
        grid_spec=pltpu.PrefetchScalarGridSpec(
            num_scalar_prefetch=1,
            grid=(1,),
            in_specs=[
                resident(grad[0]),
                resident(grad[1]),
                resident(core),
                gate_spec(mine, wide),
                gate_spec(theirs, wide),
                resident(inv),
                resident(gain),
            ],
            out_specs=resident(out),
        ),
        out_shape=out,
        compiler_params=params(),
        cost_estimate=cost(6.0),
        name="gate_dots",
    )(place, grad[0], grad[1], core, mine, theirs, inv, gain)


def recurrence_backward(place, proj, grad, start, taps, head, gain, inv, dots, kept, sizes):
    key_width, value_width = sizes
    chunks, wide = proj[0].shape[0], taps.shape[1]
    width = 2 * proj[0].shape[1]
    value = wide - 2 * key_width
    group = chunk_group(chunks, 2)
    steps = chunks // group
    order = lambda i: steps - 1 - i
    outs = [
        shape_of(*proj[0].shape, dtype=bf16),
        shape_of(*proj[1].shape, dtype=bf16),
        shape_of(8, wide),
        shape_of(chunks, 8, width),
    ]
    return pl.pallas_call(
        functools.partial(backward_kernel, group, key_width, value_width),
        grid_spec=pltpu.PrefetchScalarGridSpec(
            num_scalar_prefetch=1,
            grid=(steps,),
            in_specs=[
                spec for part in (*proj, *grad) for spec in placed_blocks(group, part, order)
            ]
            + [stepped(group, start, order)]
            + [resident(a) for a in (taps, head, gain, inv, dots)]
            + [stepped(group, a, order) for a in kept],
            out_specs=[resident(a) for a in outs],
            scratch_shapes=[
                pltpu.VMEM((key_width, value), f32),
                pltpu.VMEM((3, group, width + 8, wide), f32),
            ],
        ),
        out_shape=outs,
        compiler_params=params(),
        cost_estimate=cost(36.0 * chunks / 16),
        name="delta_backward",
    )(
        place,
        *[part for part in (*proj, *grad) for _ in range(group)],
        start,
        taps,
        head,
        gain,
        inv,
        dots,
        *kept,
    )


def weight_kernel(hidden_mine, hidden_theirs, grad_mine, grad_theirs, weight_ref, pair_ref, rest_ref, sum_ref):
    total = dot(hidden_mine[...], grad_mine[...], TN) + dot(hidden_theirs[...], grad_theirs[...], TN)
    summed = jnp.sum(total * weight_ref[...].astype(f32), axis=1, keepdims=True)
    sum_ref[...] = jnp.broadcast_to(summed, sum_ref.shape)
    low = total.astype(bf16)
    size, tiles = pair_ref.shape[2], pair_ref.shape[0]
    for block in range(pair_ref.shape[1]):
        rows = low[block * size : (block + 1) * size]
        for tile in range(tiles):
            pair_ref[tile, block] = rows[:, tile * LANES : (tile + 1) * LANES]
        for tile in range(rest_ref.shape[1] // size):
            at = (tiles + tile) * LANES
            rest_ref[block, tile * size : (tile + 1) * size] = rows[:, at : at + LANES]


def weight_gradient(hidden, grad, weight, count, tiles, rest):
    tokens, columns = grad[0].shape
    model = weight.shape[0]
    size = model // count
    step = 4 if count % 4 == 0 else 1
    part = pl.BlockSpec((tokens, step * size), lambda i: (0, i))
    whole = pl.BlockSpec((tokens, columns), lambda i: (0, 0))
    return pl.pallas_call(
        weight_kernel,
        grid=(count // step,),
        in_specs=[part, part, whole, whole, pl.BlockSpec((step * size, columns), lambda i: (i, 0))],
        out_specs=[
            pl.BlockSpec((tiles, step, size, LANES), lambda i: (0, i, 0, 0)),
            pl.BlockSpec((step, rest * size, LANES), lambda i: (i, 0, 0)),
            pl.BlockSpec((step * size, LANES), lambda i: (i, 0)),
        ],
        out_shape=[
            shape_of(tiles, count, size, LANES, dtype=bf16),
            shape_of(count, rest * size, LANES, dtype=bf16),
            shape_of(model, LANES),
        ],
        compiler_params=params(),
        cost_estimate=cost(14.0),
        name="weight_gradient",
    )(*hidden, *grad, weight)


def unpack_kernel(heads, back_ref, query_ref, key_ref, value_ref, gate_ref, out_ref):
    size = query_ref.shape[0]
    for device in range(back_ref.shape[0]):
        tiles = [back_ref[device, at : at + size].astype(f32) for at in range(0, 4 * size, size)]
        head, member = device // 4, device % 4
        pair_ref = query_ref if member < 2 else key_ref
        at = (2 * head + member % 2) * LANES
        pair_ref[:, at : at + LANES] = tiles[0]
        at = device * LANES
        value_ref[:, at : at + LANES] = tiles[1]
        gate_ref[:, at : at + LANES] = tiles[2]
        out_ref[at : at + LANES] = tiles[3]


def unpack_mixer(back, heads, shapes):
    return pl.pallas_call(
        functools.partial(unpack_kernel, heads),
        out_shape=[shape_of(*shape) for shape in shapes],
        compiler_params=params(),
        cost_estimate=cost(4.0),
        name="unpack_mixer",
    )(back)


def norm_back(grad, values, inv, gain):
    normed = values * inv
    e = grad * gain
    return inv * (e - normed * jnp.mean(e * normed, axis=-1, keepdims=True))


def on_device(
    stream_in,
    doc_start,
    first_gain,
    w_query,
    w_key,
    w_value,
    w_outgate,
    w_decay,
    w_rate,
    conv_query,
    conv_key,
    conv_value,
    a_log,
    dt_bias,
    out_gain,
    w_out,
    second_gain,
    w_gate,
    w_up,
    w_down,
    cotangent,
):
    count, pair = lax.axis_size("seq"), lax.axis_size("head")
    me, core_id = lax.axis_index("seq"), lax.axis_index("head")
    tok_rows, model = stream_in.shape
    heads = a_log.shape[0]
    members = count // heads
    head_id, member = me // members, me % members
    key_width = w_query.shape[1] // heads
    value_width = w_value.shape[1] // heads
    slice_width = value_width // members
    tokens = tok_rows * count
    rows = tok_rows // pair
    ff_slice = w_gate.shape[1] // count
    ff_full = ff_slice // LANES * LANES
    ff_wide = ff_full + LANES // 2
    ff_pack = 2 * ff_wide
    d_rows = w_query.shape[0]
    wide = 2 * key_width + LANES
    aligned = near(count) and key_width == 2 * LANES and slice_width == LANES and members == 4

    def own_rows(array):
        return lax.dynamic_slice_in_dim(array, core_id * rows, rows, 0)

    def pick(array, start, width, axis):
        return lax.dynamic_slice_in_dim(array, start, width, axis)

    place = block_places()

    stream = own_rows(stream_in).astype(f32)
    inv_one = lax.rsqrt(jnp.mean(stream * stream, axis=-1, keepdims=True) + 1e-6)
    normed_one = (stream * inv_one * first_gain).astype(bf16)
    cot_rows = own_rows(cotangent)
    own_starts = own_rows(doc_start)
    coarse = own_starts // 128
    extra = jnp.concatenate(
        [
            w_decay.reshape(rows, -1),
            w_rate.reshape(rows, -1),
            coarse.astype(bf16)[:, None],
            (own_starts - 128 * coarse).astype(bf16)[:, None],
        ],
        axis=1,
    )
    extended = jnp.concatenate([normed_one, widened(extra, LANES, 1)], axis=1)

    def gate_with_up(gate, up):
        parts = [gate[..., :ff_full], up[..., :ff_full], gate[..., ff_full:], up[..., ff_full:]]
        return jnp.concatenate(parts, axis=-1)

    def gate_and_up(both):
        split, last = both[..., : 2 * ff_full], both[..., 2 * ff_full :]
        gate = jnp.concatenate([split[..., :ff_full], last[..., : LANES // 2]], axis=-1)
        up = jnp.concatenate([split[..., ff_full:], last[..., LANES // 2 :]], axis=-1)
        return gate, up

    packed = gate_with_up(
        widened(w_gate.reshape(d_rows, count, ff_slice), ff_wide, 2),
        widened(w_up.reshape(d_rows, count, ff_slice), ff_wide, 2),
    )
    packed = jnp.swapaxes(packed.reshape(d_rows, count, -1, LANES), 0, 1)
    packed = jnp.concatenate(
        [
            jnp.swapaxes(packed, 1, 2).reshape(count, ff_pack // LANES * d_rows, LANES),
            widened(w_out.reshape(count, slice_width, -1), LANES, 2),
            widened(w_down.reshape(count, ff_slice, -1), LANES, 2),
        ],
        axis=1,
    )
    v_blocks = w_value.reshape(d_rows, count, slice_width)
    o_blocks = w_outgate.reshape(d_rows, count, slice_width)
    if aligned:
        qk = jnp.concatenate(
            [w_query.reshape(d_rows, heads, 2, LANES), w_key.reshape(d_rows, heads, 2, LANES)],
            axis=2,
        ).reshape(d_rows, count, LANES)
        qk = jnp.concatenate([qk, v_blocks, o_blocks], axis=2)
        own, packed, qk = after((gather_z(extended), packed, qk))
        sides = gather_xy(own)
        cot_own = gather_z(after(cot_rows, own[1]), PAIR)
        mixed = to_slices(qk)
        s_parts = list(exchanged(to_all(mixed[:, :LANES]))) + [mixed[:, LANES:]]
    else:
        groups = [[j * members + m for m in range(members)] for j in range(heads)]

        def whole_head(weight):
            part = to_slices(weight.reshape(d_rows, count, -1))
            return lax.all_gather(part, "seq", axis=1, tiled=True, axis_index_groups=groups)

        sides = gather_xy(gather_z(extended))
        cot_own = gather_z(cot_rows, PAIR)
        s_parts = [
            whole_head(w_query),
            whole_head(w_key),
            widened(to_slices(v_blocks), LANES, 1),
            widened(to_slices(o_blocks), LANES, 1),
        ]

    def own_taps(taps):
        return pick(taps, head_id * key_width, key_width, 1)

    taps_v = widened(pick(conv_value, me * slice_width, slice_width, 1), LANES, 1)
    taps = jnp.concatenate([own_taps(conv_query), own_taps(conv_key), taps_v], axis=1)
    taps = widened(taps, 8, 0)
    head = jnp.concatenate([-jnp.exp(pick(a_log, head_id, 1, 0)), pick(dt_bias, head_id, 1, 0)])
    head = jnp.broadcast_to(widened(head, LANES, 0)[None], (8, LANES))
    own_gain = widened(pick(out_gain, member * slice_width, slice_width, 0), LANES, 0)
    own_gain = jnp.broadcast_to(own_gain[None], (8, LANES))

    gathered = gather_end(gather_corner(sides))
    extra = [part[:, :, model:] for part in gathered]
    own_extra = extra[0] if near(count) else jnp.where(core_id == 0, extra[0], extra[1])
    own_extra = jnp.take(own_extra, place[:count], axis=0)
    thin = d_rows * heads // rows
    s_decay = own_extra[:, :, :thin].reshape(model, heads)
    s_rate = own_extra[:, :, thin : 2 * thin].reshape(model, heads)
    marks = [part[:, :, 2 * thin : 2 * thin + 2].astype(f32) for part in extra]
    marks = stream_order(marks, place)
    starts = marks[..., 0] * 128.0 + marks[..., 1]
    starts = starts - (jnp.arange(count, dtype=jnp.int32) * tok_rows).astype(f32)[:, None]
    start_cols = jnp.broadcast_to(starts[:, :, None], (count, tok_rows, 8))
    s_thin = jnp.concatenate([pick(s_decay, head_id, 1, 1), pick(s_rate, head_id, 1, 1)], axis=1)
    s_mixer = jnp.concatenate(s_parts + [widened(s_thin, LANES, 1)], axis=1)
    s_mixer, cot_own = after((s_mixer, cot_own))
    s_longer = widened(s_mixer, model + LANES, 0)

    def blocks(parts):
        return tuple(part.reshape(-1, rows, part.shape[-1]) for part in parts)

    def flat(parts):
        return tuple(part.reshape(-1, part.shape[-1]) for part in parts)

    longer_one = flat(gathered)
    proj = blocks([mm(part, s_longer) for part in longer_one])
    cot_sides = gather_xy(after(cot_own, s_mixer))
    packed = all_to_all(after(packed, s_mixer))
    core, square, *kept = recurrence_forward(place, proj, start_cols, taps, head, key_width)
    core, cot_sides, packed = after((core, cot_sides, packed))
    cot_parts = gather_corner(cot_sides)
    s_out = jnp.swapaxes(packed[:, ff_pack // LANES * d_rows :], 0, 1).reshape(-1, count * LANES)
    if LANES > w_out.shape[1]:
        s_out = jnp.swapaxes(
            packed[:, ff_pack // LANES * d_rows :, : w_out.shape[1]], 0, 1
        ).reshape(-1, model)
    s_down = widened(s_out[slice_width:], ff_wide, 0)
    s_out = widened(s_out[:slice_width], LANES, 0)
    s_ffn = from_tiles(packed[:, : ff_pack // LANES * d_rows], d_rows).reshape(model, -1)
    ffn_parts, down_parts = neighbour_slices(s_ffn, 1, ff_pack // LANES), neighbour_slices(s_down, 0, 1)

    inv_core = lax.rsqrt(sum_members(square, members) / value_width + 1e-5)
    gated = gate_forward(place, core, proj, inv_core, own_gain, wide)
    gated, ffn_parts[0] = after((gated, ffn_parts[0]))
    cot_parts = after(cot_parts, gated)
    partial, _ = scatter_begin(gated, s_out, NN)
    partial, ffn_parts[1:2] = after((partial, ffn_parts[1:2]))
    partial, _ = scatter_corner(partial)
    cot_all = gather_end(cot_parts)
    partial, ffn_parts[2:] = after((partial, ffn_parts[2:]))
    partial, _ = scatter_xy(partial)
    partial, down_parts = after((partial, down_parts))
    s_ffn, s_down = with_slices(s_ffn, ffn_parts, 1), with_slices(s_down, down_parts, 0)
    middle = stream + scatter_z(partial, rows)[0]
    inv_two = lax.rsqrt(jnp.mean(middle * middle, axis=-1, keepdims=True) + 1e-6)
    two_own = gather_z((middle * inv_two * second_gain).astype(bf16), PAIR)
    grad_inner = [mm_nt(part, s_down) for part in flat(cot_all)]
    two_own = after(two_own, grad_inner)
    hidden_two = flat(gather_end(gather_corner(gather_xy(two_own))))

    def feed_forward(hidden, grad):
        both = mm(hidden, s_ffn)
        inner, grads = [], []
        for at in range(0, both.shape[1], ff_pack):
            gate_pre, up_pre = gate_and_up(both[:, at : at + ff_pack])
            own = grad[:, at // 2 : at // 2 + ff_wide]
            sig = jax.nn.sigmoid(gate_pre)
            silu_pre = gate_pre * sig
            inner.append((silu_pre * up_pre).astype(bf16))
            grad_gate_pre = own * up_pre * sig * (1.0 + gate_pre * (1.0 - sig))
            grads.append(gate_with_up(grad_gate_pre.astype(bf16), (own * silu_pre).astype(bf16)))
        return jnp.concatenate(inner, axis=1), jnp.concatenate(grads, axis=1)

    inner, grad_gate_up = zip(*[feed_forward(*pair) for pair in zip(hidden_two, grad_inner)])
    partial, sent = scatter_begin(blocks(grad_gate_up), s_ffn, NT)
    late_two, late_inner, late_gate_up = after((hidden_two, inner, grad_gate_up), sent)
    g_ffn = sum(mm_tn(*pair) for pair in zip(late_two, late_gate_up))
    g_down = sum(mm_tn(*pair) for pair in zip(late_inner, flat(cot_all)))
    g_ffn, ffn_parts = neighbour_parts(g_ffn, 1, ff_pack // LANES)
    g_down, down_parts = neighbour_parts(g_down, 0, 1)
    partial, _ = scatter_corner(partial)
    if ffn_parts:
        partial, ffn_parts[0] = after((partial, ffn_parts[0]))
    partial, _ = scatter_xy(partial)
    if ffn_parts:
        partial, ffn_parts[1] = after((partial, ffn_parts[1]))
    grad_two, _ = scatter_z(partial, rows, PAIR)

    grad_back = norm_back(grad_two, middle, inv_two, second_gain)
    grad_middle = cot_rows.astype(f32) + grad_back
    mixer_own = gather_z(grad_middle.astype(bf16))
    late_inner = after(inner, grad_middle)
    ffn_out, _ = scatter_begin(blocks(late_inner), s_down, NN)
    mixer_sides = gather_xy(after(mixer_own, ffn_out))
    mixer_sides, ffn_parts[2:] = after((mixer_sides, ffn_parts[2:]))
    mixer_parts = gather_corner(mixer_sides)
    g_ffn = add_parts(g_ffn, ffn_parts, 1)
    mixer_parts, down_parts = after((mixer_parts, down_parts))
    g_down = add_parts(g_down, down_parts, 0)
    grad_second = jnp.sum(g_ffn * s_ffn[:, :ff_pack].astype(f32), axis=1) / second_gain
    down_tiles = jnp.swapaxes(
        g_down[:ff_slice].astype(bf16).reshape(ff_slice, count, -1), 0, 1
    )
    g_ffn = jnp.concatenate(
        [as_tiles(g_ffn.astype(bf16), count), widened(down_tiles, LANES, 2)], axis=1
    )
    g_ffn, mixer_parts, grad_second = after((g_ffn, mixer_parts, grad_second))
    grad_mixer = gather_end(mixer_parts)
    g_ffn = all_to_all(g_ffn)
    ffn_out, _ = scatter_corner(after(ffn_out, grad_mixer[0]))
    grad_mixer = flat(grad_mixer)
    grad_gated = blocks([mm_nt(part, s_out) for part in grad_mixer])
    dots = sum_members(gate_dots(place, grad_gated, core, proj, inv_core, own_gain, wide), members)
    g_out = sum(mm_tn(*pair) for pair in zip(flat(gated), grad_mixer))
    dots, ffn_out, g_out = lax.optimization_barrier((dots, ffn_out, g_out))
    ffn_out, _ = scatter_xy(ffn_out)
    *grad_proj, sums, thin_rows = recurrence_backward(
        place,
        proj,
        grad_gated,
        start_cols,
        taps,
        head,
        own_gain,
        inv_core,
        dots,
        [core] + kept,
        (key_width, value_width),
    )
    g_pairs, g_rest, g_sums = weight_gradient(
        longer_one, flat(grad_proj), s_mixer, count, 2 * key_width // LANES, 2
    )
    partial, _ = scatter_begin(after(grad_proj, g_pairs), s_mixer, NT)
    partial, sent = scatter_corner(partial)
    ffn_out, _ = scatter_z(after(ffn_out, sent), rows, PAIR)
    partial, sent_xy = scatter_xy(partial)
    grad_one, sent_z = scatter_z(partial, rows)
    g_ffn, sums, thin_rows, grad_second = after((g_ffn, sums, thin_rows, grad_second), sent_z)
    ffn_out = after(ffn_out, sent_z)
    output = both_halves((middle + ffn_out).astype(bf16))
    ff_rows = ff_pack // LANES * d_rows
    gw_down = g_ffn[:, ff_rows:, : w_down.shape[1]].reshape(w_down.shape).astype(f32)

    def joined(blocks):
        return jnp.swapaxes(blocks, 0, 1).reshape(d_rows, -1).astype(f32)

    gw_gate, gw_up = gate_and_up(from_tiles(g_ffn[:, :ff_rows], d_rows))
    gw_gate, gw_up = joined(gw_gate[..., :ff_slice]), joined(gw_up[..., :ff_slice])

    grad_input = both_halves(grad_middle + norm_back(grad_one, stream, inv_one, first_gain))

    grad_first = after(g_sums, sent_z)[:, 0] / first_gain
    if aligned:
        own = jnp.sum(exchanged(g_pairs.reshape(4, model, LANES)).astype(f32), axis=0)
        out_tiles = jnp.swapaxes(g_out.astype(bf16).reshape(LANES, count, -1), 0, 1)
        own = own.astype(bf16).reshape(count, d_rows, LANES)
        back = all_to_all(jnp.concatenate([own, g_rest, out_tiles], axis=1))
        shapes = [part.shape for part in (w_query, w_key, w_value, w_outgate, w_out)]
        gw_query, gw_key, gw_value, gw_outgate, gw_out = unpack_mixer(back, heads, shapes)
    else:

        def in_columns(tiles):
            return jnp.concatenate([tile.reshape(model, LANES) for tile in tiles], axis=1)

        def summed_slices(part):
            part = lax.psum_scatter(
                part, "seq", scatter_dimension=1, tiled=True, axis_index_groups=groups
            )
            return joined(from_slices(part, d_rows))

        out_tiles = g_out[:slice_width].astype(bf16).reshape(slice_width, count, -1)
        gw_out = all_to_all(jnp.swapaxes(out_tiles, 0, 1)).reshape(w_out.shape).astype(f32)
        half = key_width // LANES
        gw_query = summed_slices(in_columns(g_pairs[:half]))
        gw_key = summed_slices(in_columns(g_pairs[half:]))
        rest = from_tiles(g_rest, d_rows).reshape(model, 2 * LANES)
        gw_value = joined(from_slices(rest[:, :slice_width], d_rows))
        gw_outgate = joined(from_slices(rest[:, LANES : LANES + slice_width], d_rows))

    def put(part, start, width, axis):
        shape = list(part.shape)
        shape[axis] = width
        return lax.dynamic_update_slice_in_dim(jnp.zeros(shape, f32), part, start, axis)

    g_taps = sums[: conv_query.shape[0]]

    pieces = [
        put(g_taps[:, :key_width], head_id * key_width, conv_query.shape[1], 1),
        put(g_taps[:, key_width : 2 * key_width], head_id * key_width, conv_key.shape[1], 1),
        put(
            g_taps[:, 2 * key_width : 2 * key_width + slice_width],
            me * slice_width,
            conv_value.shape[1],
            1,
        ),
        put(sums[5, 0:1], head_id, heads, 0),
        put(sums[5, 1:2], head_id, heads, 0),
        put(thin_rows[None, :, :2], head_id, heads, 0),
    ]
    shared = [
        put(sums[4, :slice_width], member * slice_width, value_width, 0),
        grad_second,
        grad_first,
    ]

    def packed(parts):
        flat = jnp.concatenate([part.reshape(-1) for part in parts])
        return widened(flat, -(-flat.shape[0] // 1024) * 1024, 0).reshape(-1, LANES)

    def unpacked(flat, parts):
        flat, at, out = flat.reshape(-1), 0, []
        for part in parts:
            out.append(flat[at : at + part.size].reshape(part.shape))
            at += part.size
        return out

    merged = [packed(pieces), packed(shared)]
    summed = sum_stream(jnp.concatenate(merged, axis=0))
    cut = merged[0].shape[0]
    small = unpacked(summed[:cut], pieces)
    total = unpacked(summed[cut:] + other_core(summed[cut:]), shared)

    own_cols = blocks([pick(after(part, sent_z), me * d_rows, d_rows, 1) for part in longer_one])
    own_cols = stream_order(own_cols, place).astype(f32)
    thin_grads = jnp.einsum(
        "ctd,hcgt->gdh", own_cols, small[5], precision=lax.Precision.HIGHEST
    )
    return (
        output,
        grad_input,
        total[2],
        gw_query,
        gw_key,
        gw_value,
        gw_outgate,
        thin_grads[0],
        thin_grads[1],
        small[0],
        small[1],
        small[2],
        small[3],
        small[4],
        total[0],
        gw_out,
        total[1],
        gw_gate,
        gw_up,
        gw_down,
    )


def solution(mesh):
    in_specs = (
        P("seq", None),
        P("seq"),
        P(),
        P("seq", "head"),
        P("seq", "head"),
        P("seq", "head"),
        P("seq", "head"),
        P("seq", "head"),
        P("seq", "head"),
        P(None, "head"),
        P(None, "head"),
        P(None, "head"),
        P("head"),
        P("head"),
        P(),
        P("head", "seq"),
        P(),
        P("seq", "head"),
        P("seq", "head"),
        P("head", "seq"),
        P("seq", None),
    )
    out_specs = (
        P("seq", None),
        P("seq", None),
        P(),
        P("seq", "head"),
        P("seq", "head"),
        P("seq", "head"),
        P("seq", "head"),
        P("seq", "head"),
        P("seq", "head"),
        P(None, "head"),
        P(None, "head"),
        P(None, "head"),
        P("head"),
        P("head"),
        P(),
        P("head", "seq"),
        P(),
        P("seq", "head"),
        P("seq", "head"),
        P("head", "seq"),
    )
    return jax.shard_map(
        on_device, mesh=mesh, in_specs=in_specs, out_specs=out_specs, check_vma=False
    )
```

```python
import functools

import jax
import jax.numpy as jnp
from jax import lax
from jax.experimental import pallas as pl
from jax.experimental.pallas import tpu as pltpu
from jax.sharding import PartitionSpec as P

bf16 = jnp.bfloat16
f32 = jnp.float32
LANES = 128
VMEM_LIMIT = 56 * 2**20


def mm(left, right):
    return jnp.dot(left, right, preferred_element_type=f32)


def mm_nt(left, right):
    return lax.dot_general(left, right, (((1,), (1,)), ((), ())), preferred_element_type=f32)


def mm_tn(left, right):
    return lax.dot_general(left, right, (((0,), (0,)), ((), ())), preferred_element_type=f32)


def near(count):
    return count == 16


def across(value, offset):
    count = lax.axis_size("seq")
    return lax.ppermute(value, "seq", [(i, i ^ offset) for i in range(count)])


def other_core(value):
    return lax.ppermute(value, "head", [(0, 1), (1, 0)])


def after(value, *others):
    return lax.optimization_barrier((value, others))[0]


ALL, PAIR = (1, 2, 3), (2,)


def block_places():
    count = lax.axis_size("seq")
    blocks = jnp.arange(count, dtype=jnp.int32)
    if not near(count):
        return jnp.concatenate([blocks, jnp.zeros((1,), jnp.int32)])
    apart = blocks ^ lax.axis_index("seq")
    flip = lax.axis_index("head").astype(jnp.int32)
    return jnp.concatenate([(apart % 4) * 4 + apart // 4, flip[None]])


def gather_z(rows, zs=ALL):
    if not near(lax.axis_size("seq")):
        return [rows]
    own = rows[None]
    moved = [across(own, 4 * z) for z in zs], across(own, 1), across(own, 2)
    along_z, x_first, y_first = after(moved)
    return own, along_z, x_first, y_first


def gather_xy(state):
    if not near(lax.axis_size("seq")):
        return state
    own, along_z, x_first, y_first = state
    rest = jnp.concatenate(along_z, axis=0)
    x_rest, y_rest, corner = after((across(rest, 1), across(rest, 2), across(y_first, 1)))
    return own, rest, x_first, x_rest, y_first, y_rest, corner


def gather_corner(sides):
    if not near(lax.axis_size("seq")):
        return sides
    half = sides[1].shape[0] // 2
    x_rest, y_rest = sides[3], sides[5]
    corner = [across(y_rest[:half], 1)] if half else []
    return list(sides) + corner + [across(x_rest[half:], 2)]


def gather_end(parts):
    if not near(lax.axis_size("seq")):
        out = lax.all_gather(lax.all_gather(parts[0], "seq"), "head")
        return out[0], out[1]
    mine = jnp.concatenate(parts, axis=0)
    return mine, other_core(mine)


def scatter_begin(left, right, dims):
    blocks, rows = left[0].shape[:2]
    mine, theirs = (part.reshape(blocks * rows, -1) for part in left)

    def product(part):
        return lax.dot_general(part, right, (dims, ((), ())), preferred_element_type=f32)

    if not near(lax.axis_size("seq")):
        low = jnp.stack([product(mine), product(theirs)]).astype(bf16)
        low = lax.psum_scatter(low.reshape(2, blocks, rows, -1), "head", scatter_dimension=0)
        return low, low
    size = blocks // 2 * rows
    sent = [product(theirs[size * half : size * (half + 1)]).astype(bf16) for half in (0, 1)]
    total = [None, None]
    for half in (1, 0):
        part = product(mine[size * half : size * (half + 1)])
        total[half] = part + other_core(sent[half]).astype(f32)
    half, quarter = size // 2, size // 4
    groups = [total[group // 2][(group % 2) * half :][:half] for group in range(4)]
    return [[part[:quarter], part[quarter:]] for part in groups], sent[0]


def scatter_corner(halves, hold=()):
    if not near(lax.axis_size("seq")):
        return halves, halves
    low = [part.astype(bf16) for part in halves[3]]
    if hold:
        low[0] = after(low[0], *hold)
    mid = low[0].shape[1] // 2
    moved = [None, None]
    for half in (1, 0):
        moved[half] = across(low[half][:, :mid], 1), across(low[half][:, mid:], 2)
    return (halves, moved), low[0]


def scatter_xy(state):
    if not near(lax.axis_size("seq")):
        return state, state
    halves, moved = state
    columns = [None, None]
    for half in (1, 0):
        by_x, by_y = (part.astype(f32) for part in moved[half])
        mid = by_x.shape[1]
        y_part = halves[2][half] + jnp.pad(by_x, ((0, 0), (0, mid)))
        x_part = halves[1][half] + jnp.pad(by_y, ((0, 0), (mid, 0)))
        x_low, y_low = x_part.astype(bf16), y_part.astype(bf16)
        columns[half] = halves[0][half], across(x_low, 1), across(y_low, 2)
    return columns, y_low


def scatter_z(columns, rows, zs=ALL):
    if not near(lax.axis_size("seq")):
        return lax.psum_scatter(columns, "seq", scatter_dimension=0).astype(f32), columns
    summed = [base + x.astype(f32) + y.astype(f32) for base, x, y in columns]
    parts = [part[at : at + rows] for part in summed for at in range(0, part.shape[0], rows)]
    total = parts[0]
    for part, z in reversed(list(zip(parts[1:], zs))):
        low = part.astype(bf16)
        total = total + across(low, 4 * z).astype(f32)
    return total, low


def neighbour_slices(part, axis, cuts):
    if not near(lax.axis_size("seq")):
        return [None] * cuts
    return [across(piece, 4) for piece in jnp.split(part, cuts, axis=axis)]


def with_slices(part, pieces, axis):
    if pieces[0] is None:
        return part
    return jnp.concatenate([part] + pieces, axis=axis)


def neighbour_parts(part, axis, cuts):
    if not near(lax.axis_size("seq")):
        return part, []
    size = part.shape[axis] // 2
    mine, theirs = (lax.slice_in_dim(part, at, at + size, axis=axis) for at in (0, size))
    pieces = jnp.split(theirs.astype(bf16), cuts, axis=axis)
    return mine, [across(piece, 4) for piece in pieces]


def add_parts(mine, pieces, axis):
    if not pieces:
        return mine
    return mine + jnp.concatenate([piece.astype(f32) for piece in pieces], axis=axis)


def as_tiles(array, count):
    rows = array.shape[0] // count
    tiles = array.reshape(count, rows, -1, LANES)
    return jnp.swapaxes(tiles, 1, 2).reshape(count, -1, LANES)


def from_tiles(tiles, rows):
    count = tiles.shape[0]
    tiles = tiles.reshape(count, -1, rows, LANES)
    return jnp.swapaxes(tiles, 1, 2).reshape(count, rows, -1)


def all_to_all(blocks):
    return lax.all_to_all(blocks, "seq", split_axis=0, concat_axis=0, tiled=True)


def in_order(parts, place):
    count = parts[0].shape[0]
    return tuple(jnp.take(part, place[:count], axis=0, mode="clip") for part in parts)


def stream_order(parts, place):
    count, rows = parts[0].shape[:2]
    mine, theirs = in_order(parts, place)
    straight = place[count] == 0
    low, high = jnp.where(straight, mine, theirs), jnp.where(straight, theirs, mine)
    return jnp.concatenate([low, high], axis=1)


def both_halves(rows):
    theirs = other_core(rows)
    first = lax.axis_index("head") == 0
    return jnp.concatenate([jnp.where(first, rows, theirs), jnp.where(first, theirs, rows)], axis=0)


def sum_members(value, members):
    count = lax.axis_size("seq")
    if not near(count):
        groups = [[j * members + m for m in range(members)] for j in range(count // members)]
        return lax.psum(value, "seq", axis_index_groups=groups)
    return value + across(value, 1) + across(value, 2) + across(value, 3)


def sum_plane(value):
    if not near(lax.axis_size("seq")):
        return lax.psum(value, "seq")
    return value + across(value, 1) + across(value, 2) + across(value, 3)


def sum_column(value):
    if not near(lax.axis_size("seq")):
        return value
    return value + across(value, 4) + across(value, 8) + across(value, 12)


def to_slices(blocks):
    out = lax.all_to_all(blocks, "seq", split_axis=1, concat_axis=0, tiled=True)
    return out.reshape((-1, blocks.shape[2]))


def from_slices(grad, rows):
    blocks = grad.reshape((-1, rows, grad.shape[1]))
    return lax.all_to_all(blocks, "seq", split_axis=0, concat_axis=0, tiled=True)


def widened(array, width, axis):
    pads = [(0, 0)] * array.ndim
    pads[axis] = (0, width - array.shape[axis])
    return jnp.pad(array, pads)


def split(array):
    high = array.astype(bf16)
    return high, (array - high.astype(f32)).astype(bf16)


def dot(left, right, dims):
    return lax.dot_general(left, right, (dims, ((), ())), preferred_element_type=f32)


NN = ((1,), (0,))
NT = ((1,), (1,))
TN = ((0,), (0,))


def dot2(left, right, dims):
    high, low = split(left)
    return dot(high, right, dims) + dot(low, right, dims)


def dot3(left, right, dims):
    lh, ll = split(left)
    rh, rl = split(right)
    return dot(lh, rh, dims) + (dot(lh, rl, dims) + dot(ll, rh, dims))


def exact_sum(selector, array):
    high, low = split(array)
    rest = (array - high.astype(f32) - low.astype(f32)).astype(bf16)
    return dot(selector, high, NN) + dot(selector, low, NN) + dot(selector, rest, NN)


def square_iota(width):
    rows = lax.broadcasted_iota(jnp.int32, (width, width), 0)
    return rows, lax.broadcasted_iota(jnp.int32, (width, width), 1)


def unit_inverses(systems, width):
    rows, cols = square_iota(width)
    inverses = [jnp.where(rows == cols, 1.0, 0.0)] * len(systems)
    block = 1
    while block < width:
        mask = ((rows // block) % 2 == 1) & (cols // block == rows // block - 1)
        steps = [jnp.where(mask, system, 0.0) for system in systems]
        if block > 1:
            steps = [dot3(inverse, step, NN) for inverse, step in zip(inverses, steps)]
            steps = [dot3(step, inverse, NN) for inverse, step in zip(inverses, steps)]
        inverses = [inverse - step for inverse, step in zip(inverses, steps)]
        block *= 2
    return inverses


def in_lanes(width, *columns):
    lanes = lax.broadcasted_iota(jnp.int32, (width, LANES), 1)
    out = jnp.zeros((width, LANES), f32)
    for place, column in enumerate(columns):
        out = jnp.where(lanes == place, column, out)
    return out


def lane(array, place):
    return array[:, place : place + 1]


def as_column(row):
    return lane(jnp.broadcast_to(row, (LANES, LANES)).T, 0)


CUM, RATE, BEGIN, LOG, SOFT, START = 0, 1, 2, 3, 4, 5


def chunk_masks(width, first):
    rows, cols = square_iota(width)
    keep = (first <= cols.astype(f32)) & (rows >= cols)
    return keep, keep & (rows > cols)


def fade(width, cols, rows, start):
    first = jnp.maximum(start, 0.0)
    keep, strict = chunk_masks(width, first)
    cum = lane(cols, CUM)
    fading = jnp.exp(jnp.where(keep, cum - rows[CUM : CUM + 1], -10000.0))
    token = lax.broadcasted_iota(jnp.int32, (width, 1), 0).astype(f32)
    last = jnp.exp(jnp.where(first[width - 1 :] <= token, cum[width - 1 :] - cum, -10000.0))
    return fading, strict, last


def halves_of(low, high, flip):
    return jnp.where(flip == 0, low, high), jnp.where(flip == 0, high, low)


def whole_chunk(mine_ref, theirs_ref, place, flip):
    return jnp.concatenate(halves_of(mine_ref[place], theirs_ref[place], flip), axis=0)


def silu_back(grad, z):
    s = jax.nn.sigmoid(z)
    return grad * s * (1.0 + z * (1.0 - s))


def forward_kernel(group, key_width, mark_lane, place_ref, *refs):
    mine_refs, theirs_refs, refs = refs[:group], refs[group : 2 * group], refs[2 * group :]
    mine_extra, theirs_extra, refs = refs[:group], refs[group : 2 * group], refs[2 * group :]
    (taps_ref, head_ref, core_ref, square_ref, z_ref, q_ref, k_ref, v_ref, col_ref) = refs[:9]
    inv_ref, invk_ref, state_ref, new_ref, carry, ext = refs[9:]
    step = pl.program_id(0)
    width = core_ref.shape[1]
    wide = z_ref.shape[2]
    flip = place_ref[place_ref.shape[0] - 1]

    @pl.when(step == 0)
    def _():
        carry[...] = jnp.zeros_like(carry)
        ext[...] = jnp.zeros_like(ext)

    ext[0, 0:8] = ext[group - 1, width : width + 8]
    token = lax.broadcasted_iota(jnp.int32, (width, 1), 0).astype(f32)
    rows_id, cols_id = square_iota(width)
    triangle = jnp.where(rows_id >= cols_id, 1.0, 0.0).astype(bf16)
    own_a, bias = head_ref[0:1, 0:1], head_ref[0:1, 1:2]
    prepared = []
    for i in range(group):
        x = whole_chunk(mine_refs[i], theirs_refs[i], 0, flip)
        pre = x[:, :wide].astype(bf16).astype(f32)
        ext[i, 8 : 8 + width] = pre
        if i + 1 < group:
            ext[i + 1, 0:8] = pre[width - 8 :]
        marks = whole_chunk(mine_extra[i], theirs_extra[i], 0, flip).astype(f32)
        first = ((step * group + i) * width).astype(f32)
        start = lane(marks, mark_lane) * 128.0 + lane(marks, mark_lane + 1) - first
        z = taps_ref[0:1] * pre
        for offset in range(1, 4):
            valid = jnp.where(token - offset >= start, 1.0, 0.0)
            z = z + taps_ref[offset : offset + 1] * ext[i, 8 - offset : 8 - offset + width] * valid
        z_ref[i] = z
        conv = z * jax.nn.sigmoid(z)
        cq, ck = conv[:, :key_width], conv[:, key_width : 2 * key_width]
        q = cq * lax.rsqrt(jnp.sum(cq * cq, axis=1, keepdims=True) + 1e-6) * key_width ** (-0.5)
        k = ck * lax.rsqrt(jnp.sum(ck * ck, axis=1, keepdims=True) + 1e-6)
        q, k, v = q.astype(bf16), k.astype(bf16), conv[:, 2 * key_width :].astype(bf16)
        q_ref[i], k_ref[i], v_ref[i] = q, k, v
        soft = lane(x, x.shape[1] - LANES) + bias
        rate = jax.nn.sigmoid(lane(x, x.shape[1] - LANES + 1))
        log_decay = own_a * (jnp.maximum(soft, 0.0) + jnp.log1p(jnp.exp(-jnp.abs(soft))))
        cum = lane(exact_sum(triangle, in_lanes(width, log_decay)), 0)
        begin = jnp.where(start < 0.0, jnp.exp(cum), 0.0)
        cols = in_lanes(width, cum, rate, begin, log_decay, soft, start)
        col_ref[i] = cols
        rows = cols.T
        fading, strict, last = fade(width, cols, rows, start)
        system = jnp.where(strict, rate * dot(k, k, NT) * fading, 0.0)
        attend = dot(q, k, NT) * fading
        prepared.append((q, k, v, rows, system, attend, begin, last))
    inverses = unit_inverses([part[4] for part in prepared], width)
    solved = []
    for i in range(group):
        q, k, v, rows = prepared[i][:4]
        inv_ref[i] = inverses[i]
        scaled = inverses[i] * rows[RATE : RATE + 1]
        inv_v = dot2(scaled, v, NN)
        inv_k = dot2(scaled * rows[BEGIN : BEGIN + 1], k, NN)
        invk_ref[i] = inv_k
        solved.append((inv_v, inv_k))
    state = carry[...]
    for i in range(group):
        q, k, _, _, _, attend, begin, last = prepared[i]
        inv_v, inv_k = solved[i]
        state_ref[i] = state
        new = inv_v - dot3(inv_k, state, NN)
        new_ref[i] = new
        high, low = split(state)
        core = begin * (dot(q, high, NN) + dot(q, low, NN)) + dot3(attend, new, NN)
        core_ref[i] = core
        squares = jnp.sum(core * core, axis=1, keepdims=True)
        square_ref[pl.ds(step * group + i, 1)] = in_lanes(width, squares).T[0:1]
        high, low = split(last * new)
        state = begin[width - 1 :] * state + (dot(k, high, TN) + dot(k, low, TN))
    carry[...] = state


def gate_kernel(place_ref, core_ref, mine_ref, theirs_ref, inv_ref, gain_ref, out_mine, out_theirs):
    count, width, _ = core_ref.shape
    half = width // 2
    flip = place_ref[count]

    def step(i, _):
        place = place_ref[i]
        inv = as_column(inv_ref[pl.ds(i, 1)])
        gate = whole_chunk(mine_ref, theirs_ref, place, flip)
        gated = core_ref[i] * inv * gain_ref[0:1] * (gate * jax.nn.sigmoid(gate))
        mine, theirs = halves_of(gated[:half], gated[half:], flip)
        out_mine[place] = mine.astype(bf16)
        out_theirs[place] = theirs.astype(bf16)
        return 0

    lax.fori_loop(0, count, step, 0, unroll=4)


def dots_kernel(
    place_ref, grad_mine, grad_theirs, core_ref, mine_ref, theirs_ref, inv_ref, gain_ref, out_ref
):
    count, width, _ = core_ref.shape
    flip = place_ref[count]

    def step(i, _):
        place = place_ref[i]
        inv = as_column(inv_ref[pl.ds(i, 1)])
        gate = whole_chunk(mine_ref, theirs_ref, place, flip)
        grad = whole_chunk(grad_mine, grad_theirs, place, flip)
        e = grad * (gate * jax.nn.sigmoid(gate)) * gain_ref[0:1]
        dots = jnp.sum(e * core_ref[i] * inv, axis=1, keepdims=True)
        out_ref[pl.ds(i, 1)] = in_lanes(width, dots).T[0:1]
        return 0

    lax.fori_loop(0, count, step, 0, unroll=4)


def backward_kernel(group, low, key_width, value_width, place_ref, *refs):
    placed, refs = refs[: 4 * group], refs[4 * group :]
    mine_refs, theirs_refs = placed[:group], placed[group : 2 * group]
    grad_mine, grad_theirs = placed[2 * group : 3 * group], placed[3 * group :]
    taps_ref, head_ref, gain_ref, inv_core_ref, dots_ref = refs[:5]
    core_ref, z_ref, q_ref, k_ref, v_ref, col_ref, inv_ref, invk_ref, state_ref, new_ref = refs[5:15]
    pull_in, edge_in, sum_in, pair_ref, rest_ref, thin_ref, pull_ref, edge_ref, sum_ref = refs[15:24]
    carry, ext = refs[24:]
    step = pl.program_id(0)
    width = core_ref.shape[1]
    half = width // 2
    wide = z_ref.shape[2]
    chunks = place_ref.shape[0] - 3
    flip, apart = place_ref[chunks], place_ref[chunks + 2]
    steps = pl.num_programs(0)
    base_chunk = low + group * (steps - 1 - step)
    here = group * (steps - 1 - step)

    @pl.when(step == 0)
    def _():
        carry[...] = pull_in[...]
        sum_ref[...] = sum_in[...]
        for offset in range(3):
            ext[offset, 0, 0:8] = edge_in[offset]

    for offset in range(3):
        ext[offset, group - 1, width : width + 8] = ext[offset, 0, 0:8]
    own_a = head_ref[0:1, 0:1]
    gain = gain_ref[0:1]
    token = lax.broadcasted_iota(jnp.int32, (width, 1), 0).astype(f32)
    rows_id, cols_id = square_iota(width)
    triangle = jnp.where(rows_id <= cols_id, 1.0, 0.0).astype(bf16)
    every = range(group)
    xs = [whole_chunk(mine_refs[i], theirs_refs[i], 0, flip) for i in every]
    qs, ks = [q_ref[i] for i in every], [k_ref[i] for i in every]
    cols = [col_ref[i] for i in every]
    starts = [lane(c, START) for c in cols]
    rates, begins = [lane(c, RATE) for c in cols], [lane(c, BEGIN) for c in cols]
    fades = [fade(width, cols[i], cols[i].T, starts[i]) for i in every]
    query_key = [dot(qs[i], ks[i], NT) for i in every]
    grads, grad_gates = [], []
    for i in every:
        gate = xs[i][:, wide : wide + LANES]
        grad_gated = whole_chunk(grad_mine[i], grad_theirs[i], 0, flip)
        inv = as_column(inv_core_ref[pl.ds(base_chunk + i, 1)])
        dots = as_column(dots_ref[pl.ds(base_chunk + i, 1)])
        normed = core_ref[i] * inv
        sig = jax.nn.sigmoid(gate)
        scaled = grad_gated * (gate * sig)
        sum_ref[4:5, :LANES] += jnp.sum(scaled * normed, axis=0, keepdims=True)
        grads.append(inv * (scaled * gain - normed * (dots * (1.0 / value_width))))
        grad_gates.append(grad_gated * normed * gain * sig * (1.0 + gate * (1.0 - sig)))
    att_grads = [dot3(query_key[i] * fades[i][0], grads[i], TN) for i in every]
    bases = []
    for i in every:
        high, low = split(begins[i] * grads[i])
        bases.append((dot(qs[i], high, TN) + dot(qs[i], low, TN)) - dot3(invk_ref[i], att_grads[i], TN))
    pull = carry[...]
    pulls, grad_news = [None] * group, [None] * group
    for i in reversed(every):
        high, low = split(pull)
        back = fades[i][2] * (dot(ks[i], high, NN) + dot(ks[i], low, NN))
        pulls[i], grad_news[i] = pull, att_grads[i] + back
        pull = begins[i][width - 1 :] * pull + bases[i] - dot3(invk_ref[i], back, TN)
    carry[...] = pull
    pull_ref[...] = pull
    grad_rhs = [dot3(inv_ref[i], grad_news[i], TN) for i in every]
    grad_atts = [dot3(grads[i], new_ref[i], NT) for i in every]
    lower_fades = [jnp.where(fades[i][1], dot(ks[i], ks[i], NT) * fades[i][0], 0.0) for i in every]
    key_states, query_states = [], []
    for i in every:
        high, low = split(state_ref[i])
        key_states.append(dot(ks[i], high, NN) + dot(ks[i], low, NN))
        query_states.append(dot(qs[i], high, NN) + dot(qs[i], low, NN))
    pull_ks = [dot3(new_ref[i], pulls[i], NT) for i in every]
    systems = [jnp.where(fades[i][1], -dot3(grad_rhs[i], new_ref[i], NT), 0.0) for i in every]
    grad_vs = [rates[i] * grad_rhs[i] for i in every]
    grad_qs, grad_ks = [], []
    for i in every:
        q, k, begin, last = qs[i], ks[i], begins[i], fades[i][2]
        qh, ql = split(fades[i][0] * grad_atts[i])
        kh, kl = split(fades[i][0] * rates[i] * systems[i])
        grad_qs.append(begin * dot3(grads[i], state_ref[i], NT) + (dot(qh, k, NN) + dot(ql, k, NN)))
        grad_ks.append(
            (dot(qh, q, TN) + dot(ql, q, TN))
            + (dot(kh, k, NN) + dot(kl, k, NN))
            + (dot(kh, k, TN) + dot(kl, k, TN))
            - begin * dot3(grad_vs[i], state_ref[i], NT)
            + last * pull_ks[i]
        )
    thins = []
    for i in every:
        rate, begin, last = rates[i], begins[i], fades[i][2]
        inside = v_ref[i].astype(f32) - begin * key_states[i]
        grad_rate = jnp.sum(systems[i] * lower_fades[i], axis=1, keepdims=True) + jnp.sum(
            grad_rhs[i] * inside, axis=1, keepdims=True
        )
        grad_begin = jnp.sum(
            grads[i] * query_states[i] - grad_vs[i] * key_states[i], axis=1, keepdims=True
        )
        grad_last = jnp.sum(
            jnp.sum(pulls[i] * state_ref[i], axis=1, keepdims=True), axis=0, keepdims=True
        )
        last_part = last * jnp.sum(pull_ks[i] * ks[i].astype(f32), axis=1, keepdims=True)
        faded = grad_atts[i] * query_key[i] * fades[i][0] + rate * systems[i] * lower_fades[i]
        grad_cum = (
            jnp.sum(faded, axis=1, keepdims=True)
            - as_column(jnp.sum(faded, axis=0, keepdims=True))
            - last_part
            + grad_begin * begin
        )
        at_end = jnp.sum(last_part, axis=0, keepdims=True) + grad_last * begin[width - 1 :]
        grad_cum = grad_cum + jnp.where(token == width - 1, at_end, 0.0)
        grad_log = lane(exact_sum(triangle, in_lanes(width, grad_cum)), 0)
        log_decay, soft = lane(cols[i], LOG), lane(cols[i], SOFT)
        grad_decay = grad_log * own_a * jax.nn.sigmoid(soft)
        thin = in_lanes(width, grad_decay, grad_rate * rate * (1.0 - rate))
        thin_ref[pl.ds(here + i, 1)] = thin.T[None, 0:8]
        sum_ref[5:6, :LANES] += jnp.sum(
            in_lanes(width, grad_log * log_decay, grad_decay), axis=0, keepdims=True
        )
        thins.append(thin)
    for i in reversed(every):
        z = z_ref[i]
        sig = jax.nn.sigmoid(z)
        conv = z * sig
        cq, ck = conv[:, :key_width], conv[:, key_width : 2 * key_width]
        iq = lax.rsqrt(jnp.sum(cq * cq, axis=1, keepdims=True) + 1e-6)
        ik = lax.rsqrt(jnp.sum(ck * ck, axis=1, keepdims=True) + 1e-6)
        dq = jnp.sum(grad_qs[i] * cq, axis=1, keepdims=True)
        dk = jnp.sum(grad_ks[i] * ck, axis=1, keepdims=True)
        scale = key_width ** (-0.5)
        grad_cq = (scale * iq) * (grad_qs[i] - (iq * iq * dq) * cq)
        grad_ck = ik * (grad_ks[i] - (ik * ik * dk) * ck)
        grad_z = jnp.concatenate([grad_cq, grad_ck, grad_vs[i]], axis=1)
        grad_z = grad_z * sig * (1.0 + z * (1.0 - sig))
        pre = xs[i][:, :wide].astype(bf16).astype(f32)
        grad_pre = taps_ref[0:1] * grad_z
        sum_ref[0:1] += jnp.sum(pre * grad_z, axis=0, keepdims=True)
        for offset in range(1, 4):
            valid = jnp.where(token - offset >= starts[i], 1.0, 0.0)
            part = grad_z * valid
            ext[offset - 1, i, 0:width] = part
            if i > 0:
                ext[offset - 1, i - 1, width : width + 8] = part[0:8]
            moved = ext[offset - 1, i, offset : offset + width]
            grad_pre = grad_pre + taps_ref[offset : offset + 1] * moved
            sum_ref[offset : offset + 1] += jnp.sum(pre * moved, axis=0, keepdims=True)
        grad_pre = grad_pre.astype(bf16)
        for tile in range(pair_ref.shape[0]):
            pair_ref[tile ^ apart, i] = grad_pre[:, tile * LANES : (tile + 1) * LANES]
        rest = [grad_pre[:, 2 * key_width :], grad_gates[i].astype(bf16), thins[i].astype(bf16)]
        rest_ref[i] = jnp.concatenate(rest, axis=1)
    for offset in range(3):
        edge_ref[offset] = ext[offset, 0, 0:8]


def collect_kernel(halves, place_ref, *refs):
    refs, (out_mine, out_theirs) = list(refs[:-2]), refs[-2:]
    blocks, rows = out_mine.shape[:2]
    flip = place_ref[blocks]
    size = blocks // len(halves)
    for half, columns in enumerate(halves):
        parts = [[refs.pop(0) for _ in range(count)] for count in columns]
        for i in range(size):
            place = place_ref[half * size + i]
            at = 0
            for tiles in parts:
                total = tiles[0][i]
                if len(tiles) > 1:
                    total = sum((tile[i].astype(f32) for tile in tiles[1:]), total.astype(f32))
                mine, theirs = halves_of(total[:rows], total[rows:], flip)
                out_mine[place, :, at : at + total.shape[1]] = mine.astype(bf16)
                out_theirs[place, :, at : at + total.shape[1]] = theirs.astype(bf16)
                at += total.shape[1]


def collect(place, halves, rows):
    arrays = [array for half in halves for parts in half for array in parts]
    columns = sum(parts[0].shape[2] for parts in halves[0])
    blocks = sum(half[0][0].shape[0] for half in halves)
    out = shape_of(blocks, rows, columns, dtype=bf16)
    return pl.pallas_call(
        functools.partial(collect_kernel, [[len(parts) for parts in half] for half in halves]),
        grid_spec=pltpu.PrefetchScalarGridSpec(
            num_scalar_prefetch=1,
            grid=(1,),
            in_specs=[resident(array) for array in arrays],
            out_specs=[resident(out), resident(out)],
        ),
        out_shape=[out, out],
        compiler_params=params(),
        cost_estimate=cost(4.0),
        name="collect",
    )(place, *arrays)


def stepped(group, array, order):
    tail = array.shape[1:]
    zeros = (0,) * len(tail)
    return pl.BlockSpec((group,) + tail, lambda i, place: (order(i),) + zeros)


def resident(array):
    zeros = (0,) * len(array.shape)
    return pl.BlockSpec(array.shape, lambda i, place: zeros)


def placed_blocks(group, array, order, lanes=None):
    def spec(c):
        shape = (1, array.shape[1], array.shape[2] if lanes is None else LANES)
        return pl.BlockSpec(shape, lambda i, place: (place[group * order(i) + c], 0, lanes or 0))

    return [spec(c) for c in range(group)]


def chunk_group(chunks, most):
    return most if chunks % most == 0 else 1


def shape_of(*dims, dtype=f32):
    return jax.ShapeDtypeStruct(dims, dtype)


def cost(microseconds):
    return pl.CostEstimate(flops=0, bytes_accessed=int(microseconds * 3.6e6), transcendentals=0)


def params():
    return pltpu.CompilerParams(vmem_limit_bytes=VMEM_LIMIT)


def recurrence_forward(place, proj, gathered, taps, head, key_width, mark_lane):
    mine, theirs = proj
    extra = gathered[0].shape[2] // LANES - 1
    chunks, width, wide = mine.shape[0], 2 * mine.shape[1], taps.shape[1]
    value = wide - 2 * key_width
    group = chunk_group(chunks, 8)
    outs = [
        shape_of(chunks, width, value),
        shape_of(chunks, width),
        shape_of(chunks, width, wide),
        shape_of(chunks, width, key_width, dtype=bf16),
        shape_of(chunks, width, key_width, dtype=bf16),
        shape_of(chunks, width, value, dtype=bf16),
        shape_of(chunks, width, LANES),
        shape_of(chunks, width, width),
        shape_of(chunks, width, key_width),
        shape_of(chunks, key_width, value),
        shape_of(chunks, width, value),
    ]
    order = lambda i: i
    out_specs = [stepped(group, a, order) for a in outs]
    out_specs[1] = resident(outs[1])
    return pl.pallas_call(
        functools.partial(forward_kernel, group, key_width, mark_lane),
        grid_spec=pltpu.PrefetchScalarGridSpec(
            num_scalar_prefetch=1,
            grid=(chunks // group,),
            in_specs=placed_blocks(group, mine, order)
            + placed_blocks(group, theirs, order)
            + placed_blocks(group, gathered[0], order, extra)
            + placed_blocks(group, gathered[1], order, extra)
            + [resident(taps), resident(head)],
            out_specs=out_specs,
            scratch_shapes=[
                pltpu.VMEM((key_width, value), f32),
                pltpu.VMEM((group, width + 8, wide), f32),
            ],
        ),
        out_shape=outs,
        compiler_params=params(),
        cost_estimate=cost(28.0 * chunks / 16),
        name="delta_forward",
    )(
        place,
        *[part for part in (mine, theirs, *gathered) for _ in range(group)],
        taps,
        head,
    )


def gate_spec(proj, wide):
    shape = proj.shape[:2] + (LANES,)
    return pl.BlockSpec(shape, lambda i, place: (0, 0, wide // LANES))


def gate_forward(place, core, proj, inv, gain, wide):
    mine, theirs = proj
    out = shape_of(*mine.shape[:2], LANES, dtype=bf16)
    return pl.pallas_call(
        gate_kernel,
        grid_spec=pltpu.PrefetchScalarGridSpec(
            num_scalar_prefetch=1,
            grid=(1,),
            in_specs=[
                resident(core),
                gate_spec(mine, wide),
                gate_spec(theirs, wide),
                resident(inv),
                resident(gain),
            ],
            out_specs=[resident(out), resident(out)],
        ),
        out_shape=[out, out],
        compiler_params=params(),
        cost_estimate=cost(4.0),
        name="gate_forward",
    )(place, core, mine, theirs, inv, gain)


def gate_dots(place, grad, core, proj, inv, gain, wide):
    mine, theirs = proj
    out = shape_of(*core.shape[:2])
    return pl.pallas_call(
        dots_kernel,
        grid_spec=pltpu.PrefetchScalarGridSpec(
            num_scalar_prefetch=1,
            grid=(1,),
            in_specs=[
                resident(grad[0]),
                resident(grad[1]),
                resident(core),
                gate_spec(mine, wide),
                gate_spec(theirs, wide),
                resident(inv),
                resident(gain),
            ],
            out_specs=resident(out),
        ),
        out_shape=out,
        compiler_params=params(),
        cost_estimate=cost(6.0),
        name="gate_dots",
    )(place, grad[0], grad[1], core, mine, theirs, inv, gain)


def recurrence_backward(place, proj, grad, taps, head, gain, inv, dots, kept, sizes, state, part):
    key_width, value_width = sizes
    chunks, wide = proj[0].shape[0], taps.shape[1]
    width = 2 * proj[0].shape[1]
    value = wide - 2 * key_width
    half = chunks // 2
    group = chunk_group(half, 2)
    steps = half // group
    low = half * part
    order = lambda i: low // group + steps - 1 - i
    local = lambda i: steps - 1 - i
    if state is None:
        state = [jnp.zeros((key_width, value), f32), jnp.zeros((3, 8, wide), f32), jnp.zeros((8, wide), f32)]
    tiles = 2 * key_width // LANES
    outs = [
        shape_of(tiles, half, width, LANES, dtype=bf16),
        shape_of(half, width, 3 * LANES, dtype=bf16),
        shape_of(half, 8, width),
    ] + [shape_of(*part.shape) for part in state]
    pair_spec = pl.BlockSpec((tiles, group, width, LANES), lambda i, place: (0, local(i), 0, 0))
    *results, pull, edge, sums = pl.pallas_call(
        functools.partial(backward_kernel, group, low, key_width, value_width),
        grid_spec=pltpu.PrefetchScalarGridSpec(
            num_scalar_prefetch=1,
            grid=(steps,),
            in_specs=[
                spec for part in (*proj, *grad) for spec in placed_blocks(group, part, order)
            ]
            + [resident(a) for a in (taps, head, gain, inv, dots)]
            + [stepped(group, a, order) for a in kept]
            + [resident(a) for a in state],
            out_specs=[pair_spec, stepped(group, outs[1], local)] + [resident(a) for a in outs[2:]],
            scratch_shapes=[
                pltpu.VMEM((key_width, value), f32),
                pltpu.VMEM((3, group, width + 8, wide), f32),
            ],
        ),
        out_shape=outs,
        compiler_params=params(),
        cost_estimate=cost(18.0 * chunks / 16),
        name="delta_backward",
    )(
        place,
        *[part for part in (*proj, *grad) for _ in range(group)],
        taps,
        head,
        gain,
        inv,
        dots,
        *kept,
        *state,
    )
    return results, [pull, edge, sums]


def assemble_kernel(heads, parts, place_ref, *refs):
    part_refs, (rest_ref, extra_ref, out_ref, own_ref) = refs[:parts], refs[parts:]
    blocks, rows = extra_ref.shape[:2]
    head, apart = place_ref[blocks + 1], place_ref[blocks + 2]
    size = out_ref.shape[0] // blocks
    for part in range(parts):
        wide = part_refs[part].shape[1]
        at = pl.multiple_of((part ^ apart) * wide, LANES)
        out_ref[:, pl.ds(at, wide)] = part_refs[part][...]
    at = sum(ref.shape[1] for ref in part_refs)
    out_ref[:, at : at + rest_ref.shape[1]] = rest_ref[...]
    at += rest_ref.shape[1]
    own = part_refs[0].shape[1]
    own_ref[:, :own] = part_refs[0][...]
    own_ref[:, own : own + rest_ref.shape[1]] = rest_ref[...]
    own += rest_ref.shape[1]
    row, col = square_iota(LANES)
    fold = -(-size // rows)
    for block in range(blocks):
        x = extra_ref[place_ref[block]]
        for piece in range(fold):
            base = 2 * heads * piece + head
            pick = ((row == base) & (col == 0)) | ((row == base + heads) & (col == 1))
            thin = dot(x, jnp.where(pick, 1.0, 0.0).astype(bf16), NN).astype(bf16)
            first = block * size + piece * rows
            thin = thin[: min(rows, size)]
            out_ref[first : first + min(rows, size), at : at + LANES] = thin
            own_ref[first : first + min(rows, size), own : own + LANES] = thin


def assemble(place, parts, rest, extra, heads):
    model = rest.shape[0]
    columns = sum(part.shape[1] for part in parts) + rest.shape[1] + LANES
    own = parts[0].shape[1] + rest.shape[1] + LANES
    lanes = extra.shape[2] // LANES - 1
    return pl.pallas_call(
        functools.partial(assemble_kernel, heads, len(parts)),
        grid_spec=pltpu.PrefetchScalarGridSpec(
            num_scalar_prefetch=1,
            grid=(1,),
            in_specs=[resident(part) for part in (*parts, rest)]
            + [pl.BlockSpec(extra.shape[:2] + (LANES,), lambda i, place: (0, 0, lanes))],
            out_specs=[
                pl.BlockSpec((model, columns), lambda i, place: (0, 0)),
                pl.BlockSpec((model, own), lambda i, place: (0, 0)),
            ],
        ),
        out_shape=[shape_of(model, columns, dtype=bf16), shape_of(model, own, dtype=bf16)],
        compiler_params=params(),
        cost_estimate=cost(5.0),
        name="assemble",
    )(place, *parts, rest, extra)


def weight_kernel(hidden_mine, hidden_theirs, grad_mine, grad_theirs, weight_ref, out_ref, sum_ref):
    total = dot(hidden_mine[...], grad_mine[...], TN) + dot(hidden_theirs[...], grad_theirs[...], TN)
    summed = jnp.sum(total * weight_ref[...].astype(f32), axis=1, keepdims=True)
    sum_ref[...] = jnp.broadcast_to(summed, sum_ref.shape)
    low = total.astype(bf16)
    size = out_ref.shape[2]
    for block in range(out_ref.shape[0]):
        rows = low[block * size : (block + 1) * size]
        for tile in range(out_ref.shape[1]):
            out_ref[block, tile] = rows[:, tile * LANES : (tile + 1) * LANES]


def weight_gradient(hidden, grad, weight, count):
    tokens, columns = grad[0].shape
    model = weight.shape[0]
    size = model // count
    step = 4 if count % 4 == 0 else 1
    tiles = columns // LANES - 1
    part = pl.BlockSpec((tokens, step * size), lambda i: (0, i))
    whole = pl.BlockSpec((tokens, columns), lambda i: (0, 0))
    return pl.pallas_call(
        weight_kernel,
        grid=(count // step,),
        in_specs=[part, part, whole, whole, pl.BlockSpec((step * size, columns), lambda i: (i, 0))],
        out_specs=[
            pl.BlockSpec((step, tiles, size, LANES), lambda i: (i, 0, 0, 0)),
            pl.BlockSpec((step * size, LANES), lambda i: (i, 0)),
        ],
        out_shape=[shape_of(count, tiles, size, LANES, dtype=bf16), shape_of(model, LANES)],
        compiler_params=params(),
        cost_estimate=cost(2.0 * tiles),
        name="weight_gradient",
    )(*hidden, *grad, weight)


def unpack_kernel(tiles_ref, query_ref, key_ref, value_ref, gate_ref):
    for device in range(tiles_ref.shape[0]):
        head, member = device // 4, device % 4
        out_ref = query_ref if member < 2 else key_ref
        at = (2 * head + member % 2) * LANES
        out_ref[:, at : at + LANES] = tiles_ref[device, 0].astype(f32)
        at = device * LANES
        value_ref[:, at : at + LANES] = tiles_ref[device, 1].astype(f32)
        gate_ref[:, at : at + LANES] = tiles_ref[device, 2].astype(f32)


def unpack_mixer(tiles, shapes):
    return pl.pallas_call(
        unpack_kernel,
        out_shape=[shape_of(*shape) for shape in shapes],
        compiler_params=params(),
        cost_estimate=cost(4.0),
        name="unpack_mixer",
    )(tiles)


def unpack_ffn_kernel(ff_slice, tiles_ref, gate_ref, up_ref, down_ref, out_ref):
    size = gate_ref.shape[0]
    whole = ff_slice // LANES * LANES
    last = ff_slice - whole
    gates, ups = [], []
    for device in range(tiles_ref.shape[0]):
        full = [tiles_ref[device, at : at + size].astype(f32) for at in range(0, 2 * whole // LANES * size, size)]
        end = 2 * whole // LANES * size
        both = tiles_ref[device, end : end + size].astype(f32)
        gates += full[: len(full) // 2] + [both[:, :last]]
        ups += full[len(full) // 2 :] + [both[:, LANES // 2 : LANES // 2 + last]]
        end += size
        at = device * ff_slice
        down_ref[at : at + ff_slice] = tiles_ref[device, end : end + ff_slice].astype(f32)
        end += ff_slice
        out_ref[device * LANES : (device + 1) * LANES] = tiles_ref[device, end : end + LANES].astype(f32)
    gate_ref[...] = jnp.concatenate(gates, axis=1)
    up_ref[...] = jnp.concatenate(ups, axis=1)


def unpack_ffn(tiles, ff_slice, shapes):
    return pl.pallas_call(
        functools.partial(unpack_ffn_kernel, ff_slice),
        out_shape=[shape_of(*shape) for shape in shapes],
        compiler_params=params(),
        cost_estimate=cost(6.0),
        name="unpack_ffn",
    )(tiles)


def norm_back(grad, values, inv, gain):
    normed = values * inv
    e = grad * gain
    return inv * (e - normed * jnp.mean(e * normed, axis=-1, keepdims=True))


def on_device(
    stream_in,
    doc_start,
    first_gain,
    w_query,
    w_key,
    w_value,
    w_outgate,
    w_decay,
    w_rate,
    conv_query,
    conv_key,
    conv_value,
    a_log,
    dt_bias,
    out_gain,
    w_out,
    second_gain,
    w_gate,
    w_up,
    w_down,
    cotangent,
):
    count, pair = lax.axis_size("seq"), lax.axis_size("head")
    me, core_id = lax.axis_index("seq"), lax.axis_index("head")
    tok_rows, model = stream_in.shape
    heads = a_log.shape[0]
    members = count // heads
    head_id, member = me // members, me % members
    key_width = w_query.shape[1] // heads
    value_width = w_value.shape[1] // heads
    slice_width = value_width // members
    tokens = tok_rows * count
    rows = tok_rows // pair
    ff_slice = w_gate.shape[1] // count
    ff_full = ff_slice // LANES * LANES
    ff_wide = ff_full + LANES // 2
    ff_pack = 2 * ff_wide
    d_rows = w_query.shape[0]
    wide = 2 * key_width + LANES
    aligned = near(count) and key_width == 2 * LANES and slice_width == LANES and members == 4

    def own_rows(array):
        return lax.dynamic_slice_in_dim(array, core_id * rows, rows, 0)

    def pick(array, start, width, axis):
        return lax.dynamic_slice_in_dim(array, start, width, axis)

    place = block_places()

    stream = own_rows(stream_in).astype(f32)
    inv_one = lax.rsqrt(jnp.mean(stream * stream, axis=-1, keepdims=True) + 1e-6)
    normed_one = (stream * inv_one * first_gain).astype(bf16)
    cot_rows = own_rows(cotangent)
    own_starts = own_rows(doc_start)
    coarse = own_starts // 128
    fold = -(-d_rows // rows)
    thin_weights = widened(jnp.concatenate([w_decay, w_rate], axis=1), fold * rows, 0)
    mark_lane = 2 * heads * fold
    extra = jnp.concatenate(
        [thin_weights[at * rows : (at + 1) * rows] for at in range(fold)]
        + [coarse.astype(bf16)[:, None], (own_starts - 128 * coarse).astype(bf16)[:, None]],
        axis=1,
    )
    extended = jnp.concatenate([normed_one, widened(extra, LANES, 1)], axis=1)

    def gate_with_up(gate, up):
        parts = [gate[..., :ff_full], up[..., :ff_full], gate[..., ff_full:], up[..., ff_full:]]
        return jnp.concatenate(parts, axis=-1)

    def gate_and_up(both):
        split, last = both[..., : 2 * ff_full], both[..., 2 * ff_full :]
        gate = jnp.concatenate([split[..., :ff_full], last[..., : LANES // 2]], axis=-1)
        up = jnp.concatenate([split[..., ff_full:], last[..., LANES // 2 :]], axis=-1)
        return gate, up

    packed = gate_with_up(
        widened(w_gate.reshape(d_rows, count, ff_slice), ff_wide, 2),
        widened(w_up.reshape(d_rows, count, ff_slice), ff_wide, 2),
    )
    packed = jnp.swapaxes(packed.reshape(d_rows, count, -1, LANES), 0, 1)
    packed = jnp.concatenate(
        [
            jnp.swapaxes(packed, 1, 2).reshape(count, ff_pack // LANES * d_rows, LANES),
            widened(w_out.reshape(count, slice_width, -1), LANES, 2),
            widened(w_down.reshape(count, ff_slice, -1), LANES, 2),
        ],
        axis=1,
    )
    def own_taps(taps):
        return pick(taps, head_id * key_width, key_width, 1)

    taps_v = widened(pick(conv_value, me * slice_width, slice_width, 1), LANES, 1)
    taps = jnp.concatenate([own_taps(conv_query), own_taps(conv_key), taps_v], axis=1)
    taps = widened(taps, 8, 0)
    head = jnp.concatenate([-jnp.exp(pick(a_log, head_id, 1, 0)), pick(dt_bias, head_id, 1, 0)])
    head = jnp.broadcast_to(widened(head, LANES, 0)[None], (8, LANES))
    own_gain = widened(pick(out_gain, member * slice_width, slice_width, 0), LANES, 0)
    own_gain = jnp.broadcast_to(own_gain[None], (8, LANES))

    v_blocks = w_value.reshape(d_rows, count, slice_width)
    o_blocks = w_outgate.reshape(d_rows, count, slice_width)
    if aligned:
        qk = jnp.concatenate(
            [w_query.reshape(d_rows, heads, 2, LANES), w_key.reshape(d_rows, heads, 2, LANES)],
            axis=2,
        ).reshape(d_rows, count, LANES)
        rest = jnp.concatenate([v_blocks, o_blocks], axis=2)
        own, packed, qk, rest, taps, head, own_gain = after(
            (gather_z(extended), packed, qk, rest, taps, head, own_gain)
        )
        sides, qk = after((gather_xy(own), to_slices(qk)))
        cot_own = gather_z(after(cot_rows, own[1]), PAIR)
        s_parts = [qk] + [across(qk, offset) for offset in (1, 2, 3)]
        sides, s_parts, rest = after((sides, s_parts, rest))
        s_rest = to_slices(rest)
    else:
        groups = [[j * members + m for m in range(members)] for j in range(heads)]

        def whole_head(weight):
            part = to_slices(weight.reshape(d_rows, count, -1))
            return lax.all_gather(part, "seq", axis=1, tiled=True, axis_index_groups=groups)

        sides = gather_xy(gather_z(extended))
        cot_own = gather_z(cot_rows, PAIR)
        s_parts = [whole_head(w_query), whole_head(w_key)]
        s_rest = [widened(to_slices(part), LANES, 1) for part in (v_blocks, o_blocks)]
        s_rest = jnp.concatenate(s_rest, axis=1)

    gathered = gather_end(gather_corner(sides))
    own_extra = gathered[0]
    if not near(count):
        own_extra = jnp.where(core_id == 0, gathered[0], gathered[1])
    ids = jnp.stack([head_id, member if aligned else 0 * member]).astype(jnp.int32)
    place_ids = jnp.concatenate([place, ids])
    s_mixer, s_own = assemble(place_ids, s_parts, s_rest, own_extra, heads)
    s_own = s_own if aligned else s_mixer

    def blocks(parts):
        return tuple(part.reshape(-1, rows, part.shape[-1]) for part in parts)

    def flat(parts):
        return tuple(part.reshape(-1, part.shape[-1]) for part in parts)

    longer_one = flat(gathered)
    proj = blocks([mm(part[:, :model], s_mixer) for part in longer_one])
    packed = all_to_all(after(packed, s_rest))
    core, square, *kept = recurrence_forward(
        place, proj, gathered, taps, head, key_width, mark_lane
    )
    core, cot_own, packed = after((core, cot_own, packed))
    cot_sides = gather_xy(cot_own)
    s_out = jnp.swapaxes(packed[:, ff_pack // LANES * d_rows :], 0, 1).reshape(-1, count * LANES)
    if LANES > w_out.shape[1]:
        s_out = jnp.swapaxes(
            packed[:, ff_pack // LANES * d_rows :, : w_out.shape[1]], 0, 1
        ).reshape(-1, model)
    s_down = widened(s_out[slice_width:], ff_wide, 0)
    s_out = widened(s_out[:slice_width], LANES, 0)
    s_ffn = from_tiles(packed[:, : ff_pack // LANES * d_rows], d_rows).reshape(model, -1)
    ffn_parts, down_parts = neighbour_slices(s_ffn, 1, ff_pack // LANES), neighbour_slices(s_down, 0, 1)

    inv_core = lax.rsqrt(sum_members(square, members) / value_width + 1e-5)
    gated = gate_forward(place, core, proj, inv_core, own_gain, wide)
    gated, ffn_parts[0] = after((gated, ffn_parts[0]))
    partial, sent = scatter_begin(gated, s_out, NN)
    partial, ffn_parts[1:2] = after((partial, ffn_parts[1:2]))
    cot_parts = gather_corner(after(cot_sides, sent))
    partial, _ = scatter_corner(partial)
    cot_all = gather_end(cot_parts)
    partial, ffn_parts[2:] = after((partial, ffn_parts[2:]))
    partial, _ = scatter_xy(partial)
    partial, down_parts = after((partial, down_parts))
    middle = stream + scatter_z(partial, rows)[0]
    inv_two = lax.rsqrt(jnp.mean(middle * middle, axis=-1, keepdims=True) + 1e-6)
    two_own = gather_z((middle * inv_two * second_gain).astype(bf16), PAIR)
    s_ffn, s_down = with_slices(s_ffn, ffn_parts, 1), with_slices(s_down, down_parts, 0)
    grad_inner = [mm_nt(part, s_down) for part in flat(cot_all)]
    two_own = after(two_own, grad_inner)
    hidden_two = flat(gather_end(gather_corner(gather_xy(two_own))))

    def feed_forward(hidden, grad):
        both = mm(hidden, s_ffn)
        inner, grads = [], []
        for at in range(0, both.shape[1], ff_pack):
            gate_pre, up_pre = gate_and_up(both[:, at : at + ff_pack])
            own = grad[:, at // 2 : at // 2 + ff_wide]
            sig = jax.nn.sigmoid(gate_pre)
            silu_pre = gate_pre * sig
            inner.append((silu_pre * up_pre).astype(bf16))
            grad_gate_pre = own * up_pre * sig * (1.0 + gate_pre * (1.0 - sig))
            grads.append(gate_with_up(grad_gate_pre.astype(bf16), (own * silu_pre).astype(bf16)))
        return jnp.concatenate(inner, axis=1), jnp.concatenate(grads, axis=1)

    inner, grad_gate_up = zip(*[feed_forward(*pair) for pair in zip(hidden_two, grad_inner)])
    partial, sent = scatter_begin(blocks(grad_gate_up), s_ffn, NT)
    late_two, late_inner, late_gate_up = after((hidden_two, inner, grad_gate_up), sent)
    g_ffn = sum(mm_tn(*pair) for pair in zip(late_two, late_gate_up))
    g_down = sum(mm_tn(*pair) for pair in zip(late_inner, flat(cot_all)))
    g_ffn, ffn_parts = neighbour_parts(g_ffn, 1, ff_pack // LANES)
    g_down, down_parts = neighbour_parts(g_down, 0, 1)
    partial, _ = scatter_corner(partial)
    if ffn_parts:
        partial, ffn_parts[0] = after((partial, ffn_parts[0]))
    partial, _ = scatter_xy(partial)
    if ffn_parts:
        partial, ffn_parts[1] = after((partial, ffn_parts[1]))
    grad_two, _ = scatter_z(partial, rows, PAIR)

    grad_back = norm_back(grad_two, middle, inv_two, second_gain)
    grad_middle = cot_rows.astype(f32) + grad_back
    mixer_own = gather_z(grad_middle.astype(bf16))
    late_inner = after(inner, grad_middle)
    ffn_out, _ = scatter_begin(blocks(late_inner), s_down, NN)
    mixer_sides = gather_xy(after(mixer_own, ffn_out))
    mixer_sides, ffn_parts[2:] = after((mixer_sides, ffn_parts[2:]))
    mixer_parts = gather_corner(mixer_sides)
    g_ffn = add_parts(g_ffn, ffn_parts, 1)
    mixer_parts, down_parts = after((mixer_parts, down_parts))
    g_down = add_parts(g_down, down_parts, 0)
    grad_second = jnp.sum(g_ffn * s_ffn[:, :ff_pack].astype(f32), axis=1) / second_gain
    down_tiles = jnp.swapaxes(
        g_down[:ff_slice].astype(bf16).reshape(ff_slice, count, -1), 0, 1
    )
    ffn_tiles = [as_tiles(g_ffn.astype(bf16), count), widened(down_tiles, LANES, 2)]
    ffn_tiles, mixer_parts, grad_second = after((ffn_tiles, mixer_parts, grad_second))
    grad_mixer = gather_end(mixer_parts)
    ffn_out, _ = scatter_corner(after(ffn_out, grad_mixer[0]))
    grad_mixer = flat(grad_mixer)
    grad_gated = blocks([mm_nt(part, s_out) for part in grad_mixer])
    grad_gated, ffn_out = after((grad_gated, ffn_out))
    dots = sum_members(gate_dots(place, grad_gated, core, proj, inv_core, own_gain, wide), members)
    g_out = sum(mm_tn(*pair) for pair in zip(flat(gated), grad_mixer))
    out_tiles = jnp.swapaxes(g_out.astype(bf16)[:slice_width].reshape(slice_width, count, -1), 0, 1)
    g_ffn = jnp.concatenate(ffn_tiles + [widened(out_tiles, LANES, 2)], axis=1)
    dots, ffn_out, g_ffn = lax.optimization_barrier((dots, ffn_out, g_ffn))
    g_ffn = all_to_all(g_ffn)
    ffn_out, _ = scatter_xy(ffn_out)
    pairs = 2 * key_width // LANES
    state, halves, thin_rows = None, [None, None], [None, None]
    for part in (1, 0):
        (pair, rest, thin_rows[part]), state = recurrence_backward(
            place_ids,
            proj,
            grad_gated,
            taps,
            head,
            own_gain,
            inv_core,
            dots,
            [core] + kept,
            (key_width, value_width),
            state,
            part,
        )
        if part == 0:
            pair, halves[1], ffn_out = after((pair, halves[1], ffn_out))
        if aligned:
            tiles = [[pair[0]] + [across(pair[offset], offset) for offset in (1, 2, 3)]]
        else:
            tiles = [[pair[tile]] for tile in range(pairs)]
        halves[part] = tiles + [[rest]]
    sums = state[2]
    thin_rows = jnp.concatenate(thin_rows, axis=0)
    grad_proj = collect(place, halves, rows)
    grad_proj, g_ffn = after((grad_proj, g_ffn))
    partial, sent_core = scatter_begin(grad_proj, s_own, NT)
    partial, sent = scatter_corner(partial)
    grad_proj = after(flat(grad_proj), sent, sent_core)
    g_tiles, g_sums = weight_gradient(longer_one, grad_proj, s_own, count)
    partial, sent_xy = scatter_xy(partial)
    ffn_out, _ = scatter_z(after(ffn_out, sent_xy), rows, PAIR)
    if aligned:
        g_tiles = all_to_all(g_tiles)
    grad_first = g_sums[:, 0] / first_gain

    def put(part, start, width, axis):
        shape = list(part.shape)
        shape[axis] = width
        return lax.dynamic_update_slice_in_dim(jnp.zeros(shape, f32), part, start, axis)

    g_taps = sums[: conv_query.shape[0]]
    pieces = [
        put(g_taps[:, :key_width], head_id * key_width, conv_query.shape[1], 1),
        put(g_taps[:, key_width : 2 * key_width], head_id * key_width, conv_key.shape[1], 1),
        put(
            g_taps[:, 2 * key_width : 2 * key_width + slice_width],
            me * slice_width,
            conv_value.shape[1],
            1,
        ),
        put(sums[5, 0:1], head_id, heads, 0),
        put(sums[5, 1:2], head_id, heads, 0),
        put(thin_rows[None, :, :2], head_id, heads, 0),
    ]
    shared = [
        put(sums[4, :slice_width], member * slice_width, value_width, 0),
        grad_second,
        grad_first,
    ]

    def packed_up(parts):
        flat = jnp.concatenate([part.reshape(-1) for part in parts])
        return widened(flat, -(-flat.shape[0] // 1024) * 1024, 0).reshape(-1, LANES)

    def unpacked(flat, parts):
        flat, at, out = flat.reshape(-1), 0, []
        for part in parts:
            out.append(flat[at : at + part.size].reshape(part.shape))
            at += part.size
        return out

    merged = [packed_up(pieces), packed_up(shared)]
    summed = sum_plane(jnp.concatenate(merged, axis=0))
    grad_one, sent_z = scatter_z(partial, rows)
    summed = sum_column(summed)
    grad_one, summed = after((grad_one, summed))
    cut = merged[0].shape[0]
    small = unpacked(summed[:cut], pieces)
    total = unpacked(summed[cut:] + other_core(summed[cut:]), shared)
    g_ffn, ffn_out = after((g_ffn, ffn_out), sent_z)
    output = both_halves((middle + ffn_out).astype(bf16))
    ff_rows = ff_pack // LANES * d_rows
    down_end = ff_rows + ff_slice
    if aligned:
        shapes = [part.shape for part in (w_gate, w_up, w_down, w_out)]
        gw_gate, gw_up, gw_down, gw_out = unpack_ffn(g_ffn, ff_slice, shapes)
    else:
        gw_down = g_ffn[:, ff_rows:down_end, : w_down.shape[1]].reshape(w_down.shape).astype(f32)
        gw_out = g_ffn[:, down_end:, : w_out.shape[1]].reshape(w_out.shape).astype(f32)

    def joined(blocks):
        return jnp.swapaxes(blocks, 0, 1).reshape(d_rows, -1).astype(f32)

    if not aligned:
        gw_gate, gw_up = gate_and_up(from_tiles(g_ffn[:, :ff_rows], d_rows))
        gw_gate, gw_up = joined(gw_gate[..., :ff_slice]), joined(gw_up[..., :ff_slice])

    grad_input = both_halves(grad_middle + norm_back(grad_one, stream, inv_one, first_gain))

    if aligned:
        shapes = [part.shape for part in (w_query, w_key, w_value, w_outgate)]
        gw_query, gw_key, gw_value, gw_outgate = unpack_mixer(g_tiles, shapes)
    else:

        def in_columns(start, end):
            tiles = [g_tiles[:, tile].reshape(model, LANES) for tile in range(start, end)]
            return jnp.concatenate(tiles, axis=1)

        def summed_slices(part):
            part = lax.psum_scatter(
                part, "seq", scatter_dimension=1, tiled=True, axis_index_groups=groups
            )
            return joined(from_slices(part, d_rows))

        half = key_width // LANES
        gw_query = summed_slices(in_columns(0, half))
        gw_key = summed_slices(in_columns(half, 2 * half))
        rest = in_columns(2 * half, 2 * half + 2)
        gw_value = joined(from_slices(rest[:, :slice_width], d_rows))
        gw_outgate = joined(from_slices(rest[:, LANES : LANES + slice_width], d_rows))

    own_cols = blocks([pick(after(part, sent_z), me * d_rows, d_rows, 1) for part in longer_one])
    own_cols = stream_order(own_cols, place).astype(f32)
    thin_grads = jnp.einsum(
        "ctd,hcgt->gdh", own_cols, small[5], precision=lax.Precision.HIGHEST
    )
    return (
        output,
        grad_input,
        total[2],
        gw_query,
        gw_key,
        gw_value,
        gw_outgate,
        thin_grads[0],
        thin_grads[1],
        small[0],
        small[1],
        small[2],
        small[3],
        small[4],
        total[0],
        gw_out,
        total[1],
        gw_gate,
        gw_up,
        gw_down,
    )


def solution(mesh):
    in_specs = (
        P("seq", None),
        P("seq"),
        P(),
        P("seq", "head"),
        P("seq", "head"),
        P("seq", "head"),
        P("seq", "head"),
        P("seq", "head"),
        P("seq", "head"),
        P(None, "head"),
        P(None, "head"),
        P(None, "head"),
        P("head"),
        P("head"),
        P(),
        P("head", "seq"),
        P(),
        P("seq", "head"),
        P("seq", "head"),
        P("head", "seq"),
        P("seq", None),
    )
    out_specs = (
        P("seq", None),
        P("seq", None),
        P(),
        P("seq", "head"),
        P("seq", "head"),
        P("seq", "head"),
        P("seq", "head"),
        P("seq", "head"),
        P("seq", "head"),
        P(None, "head"),
        P(None, "head"),
        P(None, "head"),
        P("head"),
        P("head"),
        P(),
        P("head", "seq"),
        P(),
        P("seq", "head"),
        P("seq", "head"),
        P("head", "seq"),
    )
    return jax.shard_map(
        on_device, mesh=mesh, in_specs=in_specs, out_specs=out_specs, check_vma=False
    )
```
